128 devices in a mesh: hilbert: 128 (over x, z, y, core).
Axes of the slice: x: 4, y: 4, z: 4, core: 2. Of those that a mesh axis runs over, the one named last changes fastest.
Arguments:
- positions: float32 [16384, 3, 256], P('hilbert'), may hold values from 0.5 to 7.5
- masses: float32 [16384, 256], P('hilbert'), may hold values from 0.5 to 4.5
- block_owner: int32 [16384, 1], P('hilbert'), may hold values from 0 to 127, as said below
- block_oct: int32 [16384], P('hilbert'), may hold values from 0 to 63
- face_owner: int32 [8192, 6, 1], P('hilbert'), may hold values from 0 to 127, as said below
- face_oct: int32 [8192, 6], P('hilbert'), may hold values from 0 to 63
- face_coarse: int32 [8192, 6], P('hilbert'), may hold values 0 or 1
- face_quadrant: int32 [8192, 6], P('hilbert'), may hold values from 0 to 3
Outputs:
- potential: float32 [8192, 512], P('hilbert')
- accel: float32 [16384, 3, 256], P('hilbert')
The draws below stay inside these ranges and needn't reach their ends.
Inputs may be any that keep to these rules, and one draw needn't show every extreme that they name: `block_owner`: each block's owner is its own device, a device at most 4 positions away, or the device 128 / 2 positions away counted round; among the 128 blocks of one device at most 4 have any one other owner, and some other owner has exactly 4. `face_owner`: each face's neighbour owner is the face's own device, a device at most 4 positions away, or the device 128 / 2 positions away counted round; among the 384 faces of one device's octs at most 12 have a neighbour of any one other owner, and some other owner has exactly 12.
All inputs are finite; a program needn't handle non-finite values. No bound on the sum of `face_coarse` on one device may be relied on, other than what follows from the above.
Results may differ from the reference program's by a relative error of at most 0.002.
Values may be sent and summed in bfloat16 or wider, within the bound.
A program may use at most 64 MiB of HBM per device.

```python
import jax
import jax.numpy as jnp
from jax import lax

EDGE = 8
PART = 256
SWEEPS = 8
BLK_DEV = 128
OCT_DEV = 64
CAP = 4
FCAP = 12
BLOCKS = 16384
OCTS = 8192
N_HILBERT = 128


def draw_masses(key, part):
    row_ids = jnp.arange(BLOCKS).astype(jnp.float32)[:, None]
    ramp = 1.0 + 2.0 * row_ids / BLOCKS
    base = jax.random.uniform(key, (BLOCKS, PART), jnp.float32, 0.5, 1.5)
    return (base * ramp).astype(jnp.float32)


def near_owners(key, rows_dev, capacity):
    device_ids = jnp.arange(N_HILBERT, dtype=jnp.int32)
    step_table = jnp.array([1, 2, 3, 4, -1, -2, -3, -4], dtype=jnp.int32)
    near_targets = device_ids[:, None] + step_table[None, :]
    far_target = ((device_ids + N_HILBERT // 2) % N_HILBERT)[:, None]
    targets = jnp.concatenate([near_targets, far_target], axis=1).astype(jnp.int32)
    valid = (targets >= 0) & (targets < N_HILBERT)
    lane_total = 9
    count_key, pick_key, order_key = jax.random.split(key, 3)
    counts = jax.random.randint(count_key, (N_HILBERT, lane_total), 1, capacity + 1).astype(jnp.int32)
    column_ids = jnp.arange(lane_total, dtype=jnp.int32)
    scores = jax.random.randint(pick_key, (N_HILBERT, lane_total), 0, 1 << 20).astype(jnp.int32) * 16 + column_ids[None, :]
    scores = jnp.where(valid, scores, -1)
    forced = jnp.argmax(scores, axis=1).astype(jnp.int32)
    counts = jnp.where(column_ids[None, :] == forced[:, None], capacity, counts)
    counts = jnp.where(valid, counts, 0)
    ends = jnp.cumsum(counts, axis=1)
    row_ids = jnp.arange(rows_dev, dtype=jnp.int32)
    lane_ids = jnp.sum((row_ids[None, :, None] >= ends[:, None, :]).astype(jnp.int32), axis=2).astype(jnp.int32)
    order_scores = jax.random.randint(order_key, (N_HILBERT, rows_dev), 0, 1 << 16).astype(jnp.int32) * rows_dev + row_ids[None, :]
    order = jnp.argsort(order_scores, axis=1)
    shuffled = jnp.take_along_axis(lane_ids, order, axis=1)
    extended = jnp.concatenate([jnp.clip(targets, 0, N_HILBERT - 1), device_ids[:, None]], axis=1)
    return jnp.take_along_axis(extended, shuffled, axis=1).astype(jnp.int32)


def draw_block_owner(key, part):
    return near_owners(jax.random.fold_in(key, 11), BLK_DEV, CAP).reshape(BLOCKS, 1)


def draw_face_owner(key, part):
    return near_owners(jax.random.fold_in(key, 12), 6 * OCT_DEV, FCAP).reshape(OCTS, 6, 1)


def set_ends(drawn, stream_key, least, largest):
    longest = drawn.shape.index(max(drawn.shape))
    spots = []
    for shift in (0, 1):
        where = [jax.random.randint(jax.random.fold_in(stream_key, axis), (), 0, length) for axis, length in enumerate(drawn.shape)]
        where[longest] = (where[longest] + shift) % drawn.shape[longest]
        spots.append(tuple(where))
    return drawn.at[spots[0]].set(least).at[spots[1]].set(largest)


def steps_of(key, dims, cuts, least, largest):
    gain = 1.0
    for position, parts in cuts:
        heights = jax.random.uniform(jax.random.fold_in(jax.random.fold_in(key, 6), position), (parts,), jnp.float32, least / len(cuts), largest / len(cuts))
        gain = gain * jnp.repeat(jnp.exp(heights), dims[position] // parts).reshape((-1,) + (1,) * (len(dims) - 1 - position))
    return gain


def setup_inputs(seed: int = 0) -> dict:
    splits = jax.random.split(jax.random.key(seed), 9)
    return {
        "positions": jnp.clip(0.5 + 7.0 * jax.random.uniform(splits[0], (BLOCKS, 3, PART), jnp.float32) ** steps_of(splits[0], (BLOCKS, 3, PART), ((0, 128),), -0.2, 0.2), 0.5, 7.5),
        "masses": draw_masses(jax.random.fold_in(splits[8], 71), 0),
        "block_owner": draw_block_owner(jax.random.fold_in(splits[8], 71), 0),
        "block_oct": set_ends(jax.random.randint(splits[3], (BLOCKS,), 0, OCT_DEV), jax.random.fold_in(splits[3], 1), 0, OCT_DEV - 1).astype(jnp.int32),
        "face_owner": draw_face_owner(jax.random.fold_in(splits[8], 71), 0),
        "face_oct": set_ends(jax.random.randint(splits[5], (OCTS, 6), 0, OCT_DEV), jax.random.fold_in(splits[5], 1), 0, OCT_DEV - 1).astype(jnp.int32),
        "face_coarse": set_ends((jax.random.randint(splits[6], (OCTS, 6), 0, 4) < 1).astype(jnp.int32), jax.random.fold_in(splits[6], 1), 0, 1),
        "face_quadrant": set_ends(jax.random.randint(splits[7], (OCTS, 6), 0, 4), jax.random.fold_in(splits[7], 1), 0, 3).astype(jnp.int32),
    }


coupling = 0.25
group_rows = 128
highest_level = lax.Precision.HIGHEST


def cloud_weights(positions):
    centres = jnp.arange(EDGE).astype(positions.dtype) + 0.5
    return jnp.maximum(0.0, 1.0 - jnp.abs(positions[:, :, None, :] - centres[None, None, :, None]))


def cross_weights(weight_factors):
    row_count = weight_factors.shape[0]
    return (weight_factors[:, 1, :, None, :] * weight_factors[:, 2, None, :, :]).reshape(row_count, EDGE * EDGE, weight_factors.shape[3])


def deposit_block(positions, masses):
    weight_factors = cloud_weights(positions)
    crossed_faces = cross_weights(weight_factors) * masses[:, None, :]
    mesh_grid = jnp.einsum("mle,mbe->mlb", weight_factors[:, 0], crossed_faces, precision=highest_level)
    return mesh_grid.reshape(positions.shape[0], EDGE ** 3)


def interpolate_block(positions, field):
    weight_factors = cloud_weights(positions)
    crossed_faces = cross_weights(weight_factors)
    value_rows = field.astype(jnp.float32).reshape(positions.shape[0], 3, EDGE, EDGE * EDGE)
    partial_field_value = jnp.einsum("enlh,ehi->enli", value_rows, crossed_faces, precision=highest_level)
    return jnp.sum(partial_field_value * weight_factors[:, 0][:, None, :, :], axis=2)


def by_groups(action, arrays):
    row_count = arrays[0].shape[0]
    shaped = tuple(source_array.reshape((row_count // group_rows, group_rows) + source_array.shape[1:]) for source_array in arrays)
    results = lax.map(lambda members: action(*members), shaped)
    return results.reshape((row_count,) + results.shape[2:])


def face_layers(potential):
    row_count = potential.shape[0]
    face_cells = EDGE * EDGE
    x_slabs = potential.reshape(row_count, EDGE, face_cells)
    z_rods = potential.reshape(row_count, face_cells, EDGE)
    layers = [x_slabs[:, 0], x_slabs[:, EDGE - 1],
              x_slabs[:, :, :EDGE].reshape(row_count, face_cells),
              x_slabs[:, :, face_cells - EDGE:].reshape(row_count, face_cells),
              z_rods[:, :, 0], z_rods[:, :, EDGE - 1]]
    return jnp.stack(layers, axis=1)


def neighbour_pairs(potential, ghost):
    row_count = potential.shape[0]
    face_cells = EDGE * EDGE
    all_cells = EDGE ** 3
    x_up = jnp.concatenate([potential[:, face_cells:], ghost[:, 1]], axis=1)
    x_down = jnp.concatenate([ghost[:, 0], potential[:, :all_cells - face_cells]], axis=1)
    x_slabs = potential.reshape(row_count, EDGE, face_cells)
    y_up = jnp.concatenate([x_slabs[:, :, EDGE:], ghost[:, 3].reshape(row_count, EDGE, EDGE)], axis=2).reshape(row_count, all_cells)
    y_down = jnp.concatenate([ghost[:, 2].reshape(row_count, EDGE, EDGE), x_slabs[:, :, :face_cells - EDGE]], axis=2).reshape(row_count, all_cells)
    z_rods = potential.reshape(row_count, face_cells, EDGE)
    z_up = jnp.concatenate([z_rods[:, :, 1:], ghost[:, 5][:, :, None]], axis=2).reshape(row_count, all_cells)
    z_down = jnp.concatenate([ghost[:, 4][:, :, None], z_rods[:, :, :EDGE - 1]], axis=2).reshape(row_count, all_cells)
    return ((x_up, x_down), (y_up, y_down), (z_up, z_down))


def refine_table():
    cell_ids = jnp.arange(EDGE * EDGE)
    across = cell_ids // EDGE
    along = cell_ids % EDGE
    quarters = jnp.arange(4)
    half_edge = EDGE // 2
    first_idx = (quarters[:, None] // 2) * half_edge + across[None, :] // 2
    second_idx = (quarters[:, None] % 2) * half_edge + along[None, :] // 2
    return first_idx * EDGE + second_idx


def resolve_ghosts(layers, coarser, quadrant):
    table = refine_table()
    refined = jnp.take_along_axis(layers, table[quadrant], axis=1)
    return jnp.where(coarser[:, None] == 1, refined, layers)


def jacobi_sweep(potential, ghost, source):
    pairs = neighbour_pairs(potential, ghost)
    summed_partials = pairs[0][0] + pairs[0][1] + pairs[1][0] + pairs[1][1] + pairs[2][0] + pairs[2][1]
    return (summed_partials - coupling * source) / 6.0


def force_field(potential, ghost):
    pairs = neighbour_pairs(potential, ghost)
    return jnp.stack([-0.5 * (upper - lower) for upper, lower in pairs], axis=1).astype(jnp.bfloat16)


def reference(positions, masses, block_owner, block_oct, face_owner, face_oct, face_coarse, face_quadrant):
    target = (block_owner[:, 0] * OCT_DEV + block_oct).astype(jnp.int32)
    deposits = by_groups(deposit_block, (positions, masses))
    density = jax.ops.segment_sum(deposits, target, num_segments=OCTS)
    mean_density = jnp.sum(density) / (OCTS * EDGE ** 3)
    source = density - mean_density
    neighbour = (face_owner[:, :, 0] * OCT_DEV + face_oct).astype(jnp.int32)
    opposite = jnp.array([1, 0, 3, 2, 5, 4], dtype=jnp.int32)
    coarser = face_coarse.reshape(-1)
    quadrant = face_quadrant.reshape(-1)

    def ghosts(potential):
        layers = face_layers(potential)[neighbour, opposite[None, :]]
        return resolve_ghosts(layers.reshape(-1, EDGE * EDGE), coarser, quadrant).reshape(OCTS, 6, EDGE * EDGE)

    potential = jnp.zeros((OCTS, EDGE ** 3), jnp.float32)
    for sweep_round in range(SWEEPS):
        if sweep_round == 0:
            ghost = jnp.zeros((OCTS, 6, EDGE * EDGE), jnp.float32)
        else:
            ghost = ghosts(potential)
        potential = jacobi_sweep(potential, ghost, source)
    field = force_field(potential, ghosts(potential))
    accel = by_groups(lambda pos_group, oct_group: interpolate_block(pos_group, field[oct_group]), (positions, target))
    return potential, accel
```

```python
import jax
import jax.numpy as jnp
import numpy as np
from jax import lax
from jax.experimental import pallas as pl
from jax.experimental.pallas import tpu as pltpu
from jax.sharding import PartitionSpec as P

N = 128
B = 128
O = 64
C = 512
S = 64
F6 = 6 * S
PART = 256
OFFS = (1, 2, 3, 4, 127, 126, 125, 124, 64)
BACK = (4, 5, 6, 7, 0, 1, 2, 3, 8)
LANES = len(OFFS)
ROWS = 16 * LANES
TOTAL_CELLS = float(N * O * C)
COUPLING = 0.25
UNROLL = 8

f32 = jnp.float32
bf16 = jnp.bfloat16
i32 = jnp.int32


def dot(a, b):
    return jnp.dot(a, b, preferred_element_type=f32)


def dot_t(a, b):
    return lax.dot_general(a, b, (((0,), (0,)), ((), ())), preferred_element_type=f32)


def iota(shape, dim):
    return lax.broadcasted_iota(i32, shape, dim)


def static_tables():
    cell = np.arange(C)
    coords = (cell // 64, cell // 8 % 8, cell % 8)
    others = ((1, 2), (1, 2), (0, 2), (0, 2), (0, 1), (0, 1))
    pick = np.zeros((C, F6), np.float32)
    place = np.zeros((3, 256, C), np.float32)
    j = np.arange(S)
    ju, jv = j // 8, j % 8
    for f in range(6):
        own = 0 if f % 2 == 0 else 7
        x = coords[f // 2]
        u, v = coords[others[f][0]], coords[others[f][1]]
        spot = u * 8 + v
        pick[:, f * S : (f + 1) * S] = (x == 7 - own)[:, None] & (spot[:, None] == j[None, :])
        rows = slice((f % 2) * S, (f % 2 + 1) * S)
        on = (x == own)[None, :]
        place[f // 2, rows] = on & (spot[None, :] == j[:, None])
        rows = slice(128 + (f % 2) * S, 128 + (f % 2 + 1) * S)
        place[f // 2, rows] = (
            on & (u[None, :] // 2 == ju[:, None] % 4) & (v[None, :] // 2 == jv[:, None] % 4)
        )
    group = np.arange(F6) // S
    diag = (group[:, None] == group[None, :]).astype(np.float32)
    return pick, place.reshape(768, C), diag


def weights(row):
    centres = iota((8, PART), 0).astype(f32) + 0.5
    return jnp.maximum(0.0, 1.0 - jnp.abs(row - centres))


def crossed(wy, wz):
    full = jnp.concatenate([wy[y : y + 1] * wz for y in range(8)], axis=0)
    high = full.astype(bf16)
    return high, (full - high.astype(f32)).astype(bf16)


def kernel(
    pos_ref, mass_ref, block_ref, face_ref, pick_ref, place_ref, diag_ref,
    phi_ref, accel_ref,
    dep_ref, req_send, req_got, msg_send, dep_got, field_got, face_send, face_got,
    sum_send, sum_got, field_ref, dens_ref, m0_ref, mc_ref, home_ref, fmask_ref, smask_ref, gro_ref, os_ref,
    req_ss, req_rs, msg_ss, dep_rs, field_rs, face_ss, face_rs, sum_ss, sum_rs,
):
    me = lax.axis_index("hilbert")
    peers = [lax.rem(me + o, N) for o in OFFS]
    stages = []
    for stride, size in ((1, 2), (2, 4), (8, 4), (32, 4)):
        digit = lax.rem(me // stride, size)
        stages.append(
            [(me + (lax.rem(digit + j, size) - digit) * stride, size - 1 - j) for j in range(1, size)]
        )

    barrier = pltpu.get_barrier_semaphore()
    partners = peers + [p for stage in stages for p, _ in stage]
    for p in partners:
        pl.semaphore_signal(barrier, inc=1, device_id=(p,), device_id_type=pl.DeviceIdType.MESH)

    def send(src, dst, ss, rs, p):
        return pltpu.make_async_remote_copy(
            src_ref=src, dst_ref=dst, send_sem=ss, recv_sem=rs,
            device_id=(p,), device_id_type=pl.DeviceIdType.MESH,
        )

    lane128 = iota((1, 128), 1)
    offs_row = jnp.where(
        lane128 < 4,
        lane128 + 1,
        jnp.where(lane128 < 8, 131 - lane128, jnp.where(lane128 == 8, 64, -1)),
    )
    lane_f = lane128.astype(f32)

    def slots_of(match):
        rows = match.shape[0]
        earlier = (iota((rows, rows), 0) > iota((rows, rows), 1)).astype(f32).astype(bf16)
        rank = jnp.sum(dot(earlier, match.astype(bf16)) * match, axis=1, keepdims=True)
        lane = jnp.sum(match * lane_f, axis=1, keepdims=True)
        away = jnp.sum(match, axis=1, keepdims=True)
        return jnp.where(away > 0.5, lane * 16.0 + rank, -1000.0)

    face_cols = face_ref[...]
    group = iota((O, F6), 1) // S

    def spread(base):
        total = jnp.zeros((O, F6), i32)
        for f in range(6):
            total = jnp.where(group == f, face_cols[:, base + f : base + f + 1], total)
        return total

    inside = iota((O, F6), 1) % S
    delta = (face_cols[:, 0:6] - me + N) % N
    match = jnp.concatenate(
        [(delta[:, f : f + 1] == offs_row).astype(f32) for f in range(6)], axis=0
    )
    face_slot = slots_of(match)
    slot_row = iota((F6, ROWS), 1).astype(f32)
    takes = (face_slot == slot_row).astype(f32)
    gro = takes[0:O]
    for f in range(1, 6):
        gro = gro + takes[f * O : (f + 1) * O]
    gro_ref[...] = gro.astype(bf16)
    oct_col = jnp.concatenate([face_cols[:, 6 + f : 7 + f] for f in range(6)], axis=0)
    wide_lane = iota((F6, 512), 1)
    row_face = iota((F6, 512), 0) // O
    wanted = jnp.where(
        wide_lane < S,
        (oct_col == wide_lane).astype(f32),
        jnp.where(
            wide_lane < 128,
            (wide_lane - S == row_face).astype(f32),
            ((wide_lane - 128) // S == row_face).astype(f32),
        ),
    ).astype(bf16)
    asked = dot_t(takes.astype(bf16), wanted)
    smask_ref[...] = asked[:, 128:].astype(bf16)

    own_x = spread(0)
    home_ref[...] = ((own_x == me) & (spread(6) == inside)).astype(f32).astype(bf16)
    coarse_x = spread(12)
    quad_x = spread(18)
    quad_in = (inside // 32) * 2 + (inside % 8) // 4
    m0 = (coarse_x != 1).astype(f32).astype(bf16)
    mc = ((coarse_x == 1) & (quad_x == quad_in)).astype(f32).astype(bf16)
    m0_ref[...] = jnp.concatenate([m0, m0], axis=0)
    mc_ref[...] = jnp.concatenate([mc, mc], axis=0)

    block_cols = block_ref[...]
    block_delta = (block_cols[:, 0:1] - me + N) % N
    block_slot = slots_of((block_delta == offs_row).astype(f32))
    slot_lane = iota((B, ROWS), 1).astype(f32)
    into = [(block_slot + 4.0 * d == slot_lane).astype(f32).astype(bf16) for d in range(3)]
    oct_is = block_cols[:, 1:2] == iota((B, 128), 1)
    at_home = ((block_delta == 0) & oct_is).astype(f32).astype(bf16)
    oct_hot = oct_is.astype(f32).astype(bf16)
    block_oct_rows = dot_t(into[0] + into[1] + into[2], oct_hot)
    req_send[:, 0:128] = asked[:, 0:128].astype(bf16)
    req_send[:, 128:256] = block_oct_rows.astype(bf16)

    masses = mass_ref[...]
    tile = masses[0:8, 0:128]
    for r in range(16):
        for h in range(2):
            if r or h:
                tile = tile + masses[8 * r : 8 * r + 8, 128 * h : 128 * h + 128]

    pl.semaphore_wait(barrier, len(partners))

    requests = []
    for l in range(LANES):
        requests.append(
            send(
                req_send.at[pl.ds(16 * l, 16)], req_got.at[pl.ds(16 * BACK[l], 16)],
                req_ss.at[l], req_rs.at[BACK[l]], peers[l],
            )
        )
        requests[-1].start()

    def deposit(i, carry):
        for r in range(UNROLL):
            b = i * UNROLL + r
            p = pos_ref[b]
            wx = weights(p[0:1]) * mass_ref[pl.ds(b, 1), :]
            high, low = crossed(weights(p[1:2]), weights(p[2:3]))
            x_high = wx.astype(bf16).astype(f32)
            left = jnp.concatenate([x_high, wx - x_high], axis=0).astype(bf16)
            right = jnp.concatenate([high, low], axis=0)
            both = lax.dot_general(
                left, right, (((1,), (1,)), ((), ())), preferred_element_type=f32
            )
            dep_ref[pl.ds(pl.multiple_of(b * 8, 8), 8), :] = both[0:8] + both[8:16]
        return carry

    per = B // UNROLL // len(stages)
    sums = []
    n_sum = 0
    for s, stage in enumerate(stages):
        sum_send[s] = tile
        here = []
        for j, (p, back) in enumerate(stage):
            here.append(
                send(sum_send.at[s], sum_got.at[n_sum + back], sum_ss.at[n_sum + j], sum_rs.at[n_sum + back], p)
            )
            here[-1].start()
        lax.fori_loop(s * per, (s + 1) * per, deposit, 0)
        for copy in here:
            copy.wait_recv()
        for j in range(len(stage)):
            tile = tile + sum_got[n_sum + j]
        sums += here
        n_sum += len(stage)
    mean = jnp.sum(jnp.sum(tile, axis=0, keepdims=True), axis=1, keepdims=True) / TOTAL_CELLS

    low_half = iota((B, 128), 1) < S
    parts = []
    for i in range(4):
        even = dep_ref[pl.ds(2 * i, B, stride=8), :]
        odd = dep_ref[pl.ds(2 * i + 1, B, stride=8), :]
        parts.append(
            jnp.where(low_half, even + pltpu.roll(even, S, 1), odd + pltpu.roll(odd, S, 1))
        )
    rest = jnp.concatenate(parts, axis=1)
    pieces = []
    for _ in range(3):
        piece = rest.astype(bf16)
        rest = rest - piece.astype(f32)
        pieces.append(piece)
    stacked = jnp.concatenate(pieces, axis=0)
    msg_send[...] = dot_t(jnp.concatenate(into, axis=0), stacked).astype(bf16)
    deposits = []
    for l in range(LANES):
        deposits.append(
            send(
                msg_send.at[pl.ds(16 * l, 16)], dep_got.at[pl.ds(16 * BACK[l], 16)],
                msg_ss.at[l], dep_rs.at[BACK[l]], peers[l],
            )
        )
        deposits[-1].start()
    density = dot_t(jnp.concatenate([at_home] * 3, axis=0), stacked)[0:O]

    for copy in requests:
        copy.wait_recv()
    asks = req_got[...]
    os_ref[...] = asks[:, 0:S]
    to_face = (iota((128, F6), 0) - S == iota((128, F6), 1) // S).astype(f32).astype(bf16)
    fmask_ref[...] = dot(asks[:, 0:128], to_face)
    slot_octs = asks[:, 128 : 128 + S]

    for copy in deposits:
        copy.wait_recv()
    density = density + dot_t(slot_octs, dep_got[...])
    source = COUPLING * (density - mean)
    dens_ref[...] = source
    phi_ref[...] = source * (-1.0 / 6.0)

    lane = iota((1, C), 1)
    at = (lane // 64, lane // 8 % 8, lane % 8)
    strides = (64, 8, 1)

    def inner(phi, d):
        up = jnp.where(at[d] < 7, pltpu.roll(phi, C - strides[d], 1), 0.0)
        down = jnp.where(at[d] > 0, pltpu.roll(phi, strides[d], 1), 0.0)
        return up, down

    def placed(raw, d, sign):
        rows = raw.shape[0]
        part = raw[:, 128 * d : 128 * d + 128]
        if sign is not None:
            part = part * sign
        left = jnp.concatenate(
            [part * m0_ref[0:rows, 128 * d : 128 * d + 128], part * mc_ref[0:rows, 128 * d : 128 * d + 128]],
            axis=1,
        )
        return dot(left, place_ref[256 * d : 256 * d + 256, :])

    def exchange_start(phi, slot):
        high = phi.astype(bf16)
        layers = dot(high, pick_ref[...]).astype(bf16)
        chosen = dot(os_ref[...], layers) * fmask_ref[...]
        out = chosen[:, 0:128] + chosen[:, 128:256] + chosen[:, 256:384]
        face_send[...] = (out + pltpu.roll(out, S, 1)).astype(bf16)
        copies = []
        for l in range(LANES):
            copies.append(
                send(
                    face_send.at[pl.ds(16 * l, 16)], face_got.at[slot, pl.ds(16 * BACK[l], 16)],
                    face_ss.at[l], face_rs.at[slot, BACK[l]], peers[l],
                )
            )
            copies[-1].start()
        return high, layers, copies

    def home_ghosts(phi, high, layers):
        low = (phi - high.astype(f32)).astype(bf16)
        layers_low = dot(low, pick_ref[...]).astype(bf16)
        diag = diag_ref[...]
        wide = [jnp.concatenate([x] * 6, axis=0) * diag for x in (layers, layers_low)]
        return jnp.concatenate([dot(home_ref[...], x).astype(bf16) for x in wide], axis=0)

    def away_ghosts(slot):
        got = face_got[slot]
        return dot(gro_ref[...], jnp.concatenate([got] * 3, axis=1) * smask_ref[...]).astype(bf16)

    def sweep(k, carry):
        slot = lax.rem(k, 2)
        phi = phi_ref[...]
        high, layers, copies = exchange_start(phi, slot)
        raw = home_ghosts(phi, high, layers)
        total = placed(raw, 0, None) + placed(raw, 1, None) + placed(raw, 2, None)
        total = total[0:O] + total[O : 2 * O] - dens_ref[...]
        for d in range(3):
            up, down = inner(phi, d)
            total = total + (up + down)
        for copy in copies:
            copy.wait_recv()
        raw = away_ghosts(slot)
        total = total + (placed(raw, 0, None) + placed(raw, 1, None) + placed(raw, 2, None))
        phi_ref[...] = total * (1.0 / 6.0)
        for copy in copies:
            copy.wait_send()
        return carry

    lax.fori_loop(1, 8, sweep, 0)

    for copy in deposits:
        copy.wait_send()
    phi = phi_ref[...]
    high, layers, copies = exchange_start(phi, 0)
    sign = jnp.where(iota((1, 128), 1) < S, 0.5, -0.5).astype(bf16)
    raw = home_ghosts(phi, high, layers)
    near = []
    for d in range(3):
        up, down = inner(phi, d)
        part = placed(raw, d, sign)
        near.append(0.5 * (down - up) + part[0:O] + part[O : 2 * O])
    for copy in copies:
        copy.wait_recv()
    raw = away_ghosts(0)
    field = [(near[d] + placed(raw, d, sign)).astype(bf16) for d in range(3)]
    row_dim = iota((ROWS, 1), 0) % 16 // 4
    picked = [dot(slot_octs, field[d]) for d in range(3)]
    msg_send[...] = jnp.where(
        row_dim == 0, picked[0], jnp.where(row_dim == 1, picked[1], picked[2])
    ).astype(bf16)
    returns = []
    for l in range(LANES):
        returns.append(
            send(
                msg_send.at[pl.ds(16 * l, 16)], field_got.at[pl.ds(16 * BACK[l], 16)],
                msg_ss.at[l], field_rs.at[BACK[l]], peers[l],
            )
        )
        returns[-1].start()
    mine = [dot(at_home[:, 0:O], field[d]) for d in range(3)]
    for copy in returns:
        copy.wait_recv()
    got = field_got[...]
    for d in range(3):
        values = mine[d] + dot(into[d], got)
        for i in range(4):
            pair = values[:, 128 * i : 128 * i + 128]
            turned = pltpu.roll(pair, S, 1)
            field_ref[d, pl.ds(2 * i, B, stride=8), :] = jnp.where(low_half, pair, turned)
            field_ref[d, pl.ds(2 * i + 1, B, stride=8), :] = jnp.where(low_half, turned, pair)

    def interpolate(i, carry):
        for r in range(UNROLL):
            b = i * UNROLL + r
            p = pos_ref[b]
            wx = weights(p[0:1])
            high, low = crossed(weights(p[1:2]), weights(p[2:3]))
            rows = pl.ds(pl.multiple_of(b * 8, 8), 8)
            left = jnp.concatenate([field_ref[d, rows, :] for d in range(3)], axis=0).astype(bf16)
            value = dot(left, jnp.concatenate([high, low], axis=0))
            accel_ref[b] = jnp.concatenate(
                [jnp.sum(value[8 * d : 8 * d + 8] * wx, axis=0, keepdims=True) for d in range(3)],
                axis=0,
            )
        return carry

    lax.fori_loop(0, B // UNROLL, interpolate, 0)

    for copy in requests + sums + copies + returns:
        copy.wait_send()


def on_device(
    positions, masses, block_owner, block_oct, face_owner, face_oct, face_coarse, face_quadrant
):
    blocks = jnp.concatenate([block_owner, block_oct[:, None]], axis=1)
    faces = jnp.concatenate([face_owner[:, :, 0], face_oct, face_coarse, face_quadrant], axis=1)
    pick, place, diag = static_tables()
    dma = pltpu.SemaphoreType.DMA
    vmem = pl.BlockSpec(memory_space=pltpu.VMEM)
    return pl.pallas_call(
        kernel,
        out_shape=(
            jax.ShapeDtypeStruct((O, C), f32),
            jax.ShapeDtypeStruct((B, 3, PART), f32),
        ),
        in_specs=[vmem] * 7,
        out_specs=(vmem, vmem),
        scratch_shapes=[
            pltpu.VMEM((B * 8, 128), f32),
            pltpu.VMEM((ROWS, 256), bf16),
            pltpu.VMEM((ROWS, 256), bf16),
            pltpu.VMEM((ROWS, C), bf16),
            pltpu.VMEM((ROWS, C), bf16),
            pltpu.VMEM((ROWS, C), bf16),
            pltpu.VMEM((ROWS, 128), bf16),
            pltpu.VMEM((2, ROWS, 128), bf16),
            pltpu.VMEM((4, 8, 128), f32),
            pltpu.VMEM((10, 8, 128), f32),
            pltpu.VMEM((3, B * 8, 128), f32),
            pltpu.VMEM((O, C), f32),
            pltpu.VMEM((2 * O, F6), bf16),
            pltpu.VMEM((2 * O, F6), bf16),
            pltpu.VMEM((O, F6), bf16),
            pltpu.VMEM((ROWS, F6), f32),
            pltpu.VMEM((ROWS, F6), bf16),
            pltpu.VMEM((O, ROWS), bf16),
            pltpu.VMEM((ROWS, S), bf16),
            dma((LANES,)),
            dma((LANES,)),
            dma((LANES,)),
            dma((LANES,)),
            dma((LANES,)),
            dma((LANES,)),
            dma((2, LANES)),
            dma((10,)),
            dma((10,)),
        ],
        compiler_params=pltpu.CompilerParams(
            collective_id=0, has_side_effects=True, vmem_limit_bytes=40 * 1024 * 1024
        ),
    )(
        positions,
        masses,
        blocks,
        faces,
        jnp.asarray(pick, bf16),
        jnp.asarray(place, bf16),
        jnp.asarray(diag, bf16),
    )


def solution(mesh):
    placed = (
        P("hilbert", None, None),
        P("hilbert", None),
        P("hilbert", None),
        P("hilbert"),
        P("hilbert", None, None),
        P("hilbert", None),
        P("hilbert", None),
        P("hilbert", None),
    )
    return jax.shard_map(
        on_device,
        mesh=mesh,
        in_specs=placed,
        out_specs=(P("hilbert", None), P("hilbert", None, None)),
        check_vma=False,
    )
```

```python
import jax
import jax.numpy as jnp
from jax import lax
from jax.experimental import pallas as pl
from jax.experimental.pallas import tpu as pltpu
from jax.sharding import PartitionSpec as P

N = 128
B = 128
O = 64
C = 512
S = 64
F6 = 6 * S
PART = 256
OFFS = (1, 2, 3, 4, 127, 126, 125, 124, 64)
BACK = (4, 5, 6, 7, 0, 1, 2, 3, 8)
LANES = len(OFFS)
LANE_ORDER = (8, 3, 7, 2, 6, 1, 5, 0, 4)
ROWS = 16 * LANES
TOTAL_CELLS = float(N * O * C)
COUPLING = 0.25

f32 = jnp.float32
bf16 = jnp.bfloat16
i32 = jnp.int32


def dot(a, b):
    return jnp.dot(a, b, preferred_element_type=f32)


def dot_t(a, b):
    return lax.dot_general(a, b, (((0,), (0,)), ((), ())), preferred_element_type=f32)


def iota(shape, dim):
    return lax.broadcasted_iota(i32, shape, dim)


def pick_table(d):
    cell, lane = iota((C, 128), 0), iota((C, 128), 1)
    coord, spot = cell_spot(cell, d)
    return ((coord == jnp.where(lane < S, 7, 0)) & (spot == lane % S)).astype(f32).astype(bf16)


def place_table(d):
    row, cell = iota((256, C), 0), iota((256, C), 1)
    coord, spot = cell_spot(cell, d)
    j = row % S
    here = coord == (row // S % 2) * 7
    fine = spot == j
    coarse = ((spot // 16) == (j // 8 % 4)) & ((spot % 8) // 2 == j % 4)
    return (here & (((row < 128) & fine) | ((row >= 128) & coarse))).astype(f32).astype(bf16)


def cell_spot(cell, d):
    x, y, z = cell // 64, cell // 8 % 8, cell % 8
    return ((x, y * 8 + z), (y, x * 8 + z), (z, x * 8 + y))[d]


def weights(row):
    centres = iota((8, PART), 0).astype(f32) + 0.5
    return jnp.maximum(0.0, 1.0 - jnp.abs(row - centres))


def crossed(wy, wz):
    full = jnp.concatenate([wy[y : y + 1] * wz for y in range(8)], axis=0)
    high = full.astype(bf16)
    return high, (full - high.astype(f32)).astype(bf16)


def device_at(x, z, y, core):
    return x * 32 + z * 8 + y * 2 + core


def host_of(i):
    x, z, y = i // 32, lax.rem(i // 8, 4), lax.rem(i // 2, 4)
    return device_at(
        lax.rem(x + 3, 4),
        z + lax.rem(x, 2) * (3 - 2 * z),
        y + lax.rem(z, 2) * (3 - 2 * y),
        lax.rem(i, 2),
    )


def hosted_by(i):
    x, z, y = lax.rem(i // 32 + 1, 4), lax.rem(i // 8, 4), lax.rem(i // 2, 4)
    z = z + lax.rem(x, 2) * (3 - 2 * z)
    return device_at(x, z, y + lax.rem(z, 2) * (3 - 2 * y), lax.rem(i, 2))


def kernel(
    pos_ref, mass_ref, bown_ref, boct_ref, fown_ref, foct_ref, fco_ref, fq_ref,
    phi_ref, accel_ref,
    dep_ref, req_send, req_got, msg_send, dep_got, field_got, face_send, face_got,
    sum_send, sum_got, field_ref, dens_ref, m0_ref, mc_ref, home_ref, fmask_ref, smask_ref, gro_ref, os_ref,
    pick_ref, place_ref, diag_ref, index_ref, index_got, home_send, home_got, fhome_send, fhome_got,
    work_ref, phi_got,
    req_ss, req_rs, msg_ss, dep_rs, field_rs, face_ss, face_rs, sum_ss, sum_rs, one_ss, one_rs,
):
    me = lax.axis_index("hilbert")
    owner = hosted_by(me)
    my_host = host_of(me)
    near = [lax.rem(me + o, N) for o in OFFS]
    hosts = [host_of(p) for p in near]
    holders = [lax.rem(owner + o, N) for o in OFFS]
    peers = [host_of(p) for p in holders]
    stages = []
    for stride, size in ((1, 2), (2, 4), (8, 4), (32, 4)):
        digit = lax.rem(me // stride, size)
        stages.append(
            [(me + (lax.rem(digit + j, size) - digit) * stride, size - 1 - j) for j in range(1, size)]
        )
    first_sum = (0, 1, 4, 7)

    barrier = pltpu.get_barrier_semaphore()
    partners = peers + hosts + holders + [my_host, owner] + [p for stage in stages for p, _ in stage]
    for p in partners:
        pl.semaphore_signal(barrier, inc=1, device_id=(p,), device_id_type=pl.DeviceIdType.MESH)

    def send(src, dst, ss, rs, p):
        copy = pltpu.make_async_remote_copy(
            src_ref=src, dst_ref=dst, send_sem=ss, recv_sem=rs,
            device_id=(p,), device_id_type=pl.DeviceIdType.MESH,
        )
        copy.start()
        return copy

    def send_lanes(src, dst, ss, rs, to):
        return [
            send(
                src.at[pl.ds(16 * l, 16)], dst.at[pl.ds(16 * BACK[l], 16)],
                ss.at[l], rs.at[BACK[l]], to[l],
            )
            for l in LANE_ORDER
        ]

    lane128 = iota((1, 128), 1)
    offs_row = jnp.where(
        lane128 < 4,
        lane128 + 1,
        jnp.where(lane128 < 8, 131 - lane128, jnp.where(lane128 == 8, 64, -1)),
    )
    lane_f = lane128.astype(f32)

    def slots_of(match):
        rows = match.shape[0]
        earlier = (iota((rows, rows), 0) > iota((rows, rows), 1)).astype(f32).astype(bf16)
        rank = jnp.sum(dot(earlier, match.astype(bf16)) * match, axis=1, keepdims=True)
        lane = jnp.sum(match * lane_f, axis=1, keepdims=True)
        away = jnp.sum(match, axis=1, keepdims=True)
        return jnp.where(away > 0.5, lane * 16.0 + rank, -1000.0)

    def face_slots(columns, of):
        delta = (columns[0:O, 0:6] - of + N) % N
        match = jnp.concatenate(
            [(delta[:, f : f + 1] == offs_row).astype(f32) for f in range(6)], axis=0
        )
        return (slots_of(match) == iota((F6, ROWS), 1).astype(f32)).astype(f32)

    index_ref[...] = jnp.zeros((128, 128), f32)
    for f in range(6):
        index_ref[f : f + 1, 0:O] = fown_ref[f].astype(f32)
        index_ref[8 + f : 9 + f, 0:O] = foct_ref[f : f + 1].astype(f32)
        index_ref[16 + f : 17 + f, 0:O] = fco_ref[f : f + 1].astype(f32)
        index_ref[24 + f : 25 + f, 0:O] = fq_ref[f : f + 1].astype(f32)
    index_ref[32:33, :] = bown_ref[...].astype(f32)
    index_ref[33:34, :] = boct_ref[...].astype(f32)
    columns = index_ref[...].T.astype(i32)

    takes = face_slots(columns, me)
    oct_col = jnp.concatenate([columns[0:O, 8 + f : 9 + f] for f in range(6)], axis=0)
    lane_wide = iota((F6, 128), 1)
    row_face = iota((F6, 128), 0) // O
    wanted = jnp.where(
        lane_wide < S, (oct_col == lane_wide).astype(f32), (lane_wide - S == row_face).astype(f32)
    ).astype(bf16)

    block_delta = (columns[:, 32:33] - me + N) % N
    block_slot = slots_of((block_delta == offs_row).astype(f32))
    slot_lane = iota((B, ROWS), 1).astype(f32)
    into = [(block_slot + 4.0 * d == slot_lane).astype(f32).astype(bf16) for d in range(3)]
    oct_is = columns[:, 33:34] == iota((B, 128), 1)
    at_home = ((block_delta == 0) & oct_is).astype(f32).astype(bf16)
    oct_hot = oct_is.astype(f32).astype(bf16)
    req_send[:, 0:128] = dot_t(takes.astype(bf16), wanted).astype(bf16)
    req_send[:, 128:256] = dot_t(into[0] + into[1] + into[2], oct_hot).astype(bf16)

    masses = mass_ref[...]
    tile = masses[0:8, 0:128]
    for r in range(16):
        for h in range(2):
            if r or h:
                tile = tile + masses[8 * r : 8 * r + 8, 128 * h : 128 * h + 128]

    def deposit(i, carry):
        rows = pl.ds(pl.multiple_of(i * 8, 8), 8)
        xs, ys, zs, ms = pos_ref[0, rows, :], pos_ref[1, rows, :], pos_ref[2, rows, :], mass_ref[rows, :]
        for r in range(8):
            wx = weights(xs[r : r + 1]) * ms[r : r + 1]
            high, low = crossed(weights(ys[r : r + 1]), weights(zs[r : r + 1]))
            x_high = wx.astype(bf16).astype(f32)
            left = jnp.concatenate([x_high, wx - x_high], axis=0).astype(bf16)
            right = jnp.concatenate([high, low], axis=0)
            both = lax.dot_general(
                left, right, (((1,), (1,)), ((), ())), preferred_element_type=f32
            )
            dep_ref[pl.ds(pl.multiple_of(i * 64 + 8 * r, 8), 8), :] = both[0:8] + both[8:16]
        return carry

    lax.fori_loop(0, B // 8, deposit, 0)

    low_half = iota((B, 128), 1) < S
    parts = []
    for i in range(4):
        even = dep_ref[pl.ds(2 * i, B, stride=8), :]
        odd = dep_ref[pl.ds(2 * i + 1, B, stride=8), :]
        parts.append(
            jnp.where(low_half, even + pltpu.roll(even, S, 1), odd + pltpu.roll(odd, S, 1))
        )
    rest = jnp.concatenate(parts, axis=1)
    pieces = []
    for _ in range(3):
        piece = rest.astype(bf16)
        rest = rest - piece.astype(f32)
        pieces.append(piece)
    stacked = jnp.concatenate(pieces, axis=0)
    home_send[...] = dot_t(jnp.concatenate([at_home] * 3, axis=0), stacked)[0:O]
    msg_send[...] = dot_t(jnp.concatenate(into, axis=0), stacked).astype(bf16)

    pl.semaphore_wait(barrier, len(partners))

    index_copy = send(index_ref.at[pl.ds(0, 32)], index_got, one_ss.at[0], one_rs.at[0], my_host)
    home_copy = send(home_send, home_got, one_ss.at[1], one_rs.at[1], my_host)
    deposits = send_lanes(msg_send, dep_got, msg_ss, dep_rs, hosts)
    requests = send_lanes(req_send, req_got, req_ss, req_rs, hosts)
    sums = []

    def sum_start(s, tile):
        sum_send[s] = tile
        for j, (p, back) in enumerate(stages[s]):
            at = first_sum[s]
            sums.append(
                send(sum_send.at[s], sum_got.at[at + back], sum_ss.at[at + j], sum_rs.at[at + back], p)
            )

    def sum_end(s, tile):
        at, count = first_sum[s], len(stages[s])
        for copy in sums[at : at + count]:
            copy.wait_recv()
        for j in range(count):
            tile = tile + sum_got[at + j]
        return tile

    sum_start(0, tile)

    for d in range(3):
        pick_ref[:, 128 * d : 128 * d + 128] = pick_table(d)
        place_ref[256 * d : 256 * d + 256, :] = place_table(d)
    diag_ref[...] = (iota((F6, F6), 0) // S == iota((F6, F6), 1) // S).astype(f32).astype(bf16)
    to_face = (iota((128, F6), 0) - S == iota((128, F6), 1) // S).astype(f32).astype(bf16)

    tile = sum_end(0, tile)
    sum_start(1, tile)

    index_copy.wait_recv()
    spare = jnp.zeros((96, 128), f32)
    columns = jnp.concatenate([index_got[...], spare], axis=0).T.astype(i32)
    group = iota((O, F6), 1) // S

    def spread(base):
        total = jnp.zeros((O, F6), i32)
        for f in range(6):
            total = jnp.where(group == f, columns[0:O, base + f : base + f + 1], total)
        return total

    takes = face_slots(columns, owner)
    gro = takes[0:O]
    for f in range(1, 6):
        gro = gro + takes[f * O : (f + 1) * O]
    gro_ref[...] = gro.astype(bf16)
    same_face = (iota((F6, F6), 0) // O == iota((F6, F6), 1) // S).astype(f32).astype(bf16)
    smask_ref[...] = dot_t(takes.astype(bf16), same_face).astype(bf16)
    inside = iota((O, F6), 1) % S
    home_ref[...] = ((spread(0) == owner) & (spread(8) == inside)).astype(f32).astype(bf16)
    coarse_x = spread(16)
    quad_x = spread(24)
    quad_in = (inside // 32) * 2 + (inside % 8) // 4
    m0 = (coarse_x != 1).astype(f32).astype(bf16)
    mc = ((coarse_x == 1) & (quad_x == quad_in)).astype(f32).astype(bf16)
    m0_ref[...] = jnp.concatenate([m0, m0], axis=0)
    mc_ref[...] = jnp.concatenate([mc, mc], axis=0)

    for copy in requests:
        copy.wait_recv()
    asks = req_got[...]
    os_ref[...] = asks[:, 0:S]
    fmask_ref[...] = dot(asks[:, 0:128], to_face)
    slot_octs = asks[:, 128 : 128 + S]

    for copy in deposits:
        copy.wait_recv()
    density = dot_t(slot_octs, dep_got[...])
    home_copy.wait_recv()
    source = COUPLING * (density + home_got[...])
    dens_ref[...] = source
    work_ref[...] = source * (-1.0 / 6.0)

    lane = iota((1, C), 1)
    at = (lane // 64, lane // 8 % 8, lane % 8)
    strides = (64, 8, 1)

    def inner(phi, d):
        up = jnp.where(at[d] < 7, pltpu.roll(phi, C - strides[d], 1), 0.0)
        down = jnp.where(at[d] > 0, pltpu.roll(phi, strides[d], 1), 0.0)
        return up, down

    def placed(raw, d, sign):
        rows = raw.shape[0]
        part = raw[:, 128 * d : 128 * d + 128]
        if sign is not None:
            part = part * sign
        left = jnp.concatenate(
            [part * m0_ref[0:rows, 128 * d : 128 * d + 128], part * mc_ref[0:rows, 128 * d : 128 * d + 128]],
            axis=1,
        )
        return dot(left, place_ref[256 * d : 256 * d + 256, :])

    def exchange_start(phi, slot):
        high = phi.astype(bf16)
        layers = dot(high, pick_ref[...]).astype(bf16)
        chosen = dot(os_ref[...], layers) * fmask_ref[...]
        out = chosen[:, 0:128] + chosen[:, 128:256] + chosen[:, 256:384]
        face_send[...] = (out + pltpu.roll(out, S, 1)).astype(bf16)
        copies = send_lanes(face_send, face_got.at[slot], face_ss, face_rs.at[slot], peers)
        return high, layers, copies

    def home_ghosts(phi, high, layers):
        low = (phi - high.astype(f32)).astype(bf16)
        layers_low = dot(low, pick_ref[...]).astype(bf16)
        diag = diag_ref[...]
        wide = [jnp.concatenate([x] * 6, axis=0) * diag for x in (layers, layers_low)]
        return jnp.concatenate([dot(home_ref[...], x).astype(bf16) for x in wide], axis=0)

    def away_ghosts(slot):
        got = face_got[slot]
        return dot(gro_ref[...], jnp.concatenate([got] * 3, axis=1) * smask_ref[...]).astype(bf16)

    def sweep(slot, between):
        phi = work_ref[...]
        high, layers, copies = exchange_start(phi, slot)
        between()
        raw = home_ghosts(phi, high, layers)
        total = placed(raw, 0, None) + placed(raw, 1, None) + placed(raw, 2, None)
        total = total[0:O] + total[O : 2 * O] - dens_ref[...]
        for d in range(3):
            up, down = inner(phi, d)
            total = total + (up + down)
        for copy in copies:
            copy.wait_recv()
        raw = away_ghosts(slot)
        total = total + (placed(raw, 0, None) + placed(raw, 1, None) + placed(raw, 2, None))
        work_ref[...] = total * (1.0 / 6.0)
        for copy in copies:
            copy.wait_send()

    tiles = [tile]

    def step_sum(s):
        tiles.append(sum_end(s, tiles[-1]))
        if s < 3:
            sum_start(s + 1, tiles[-1])

    for k in range(1, 4):
        sweep(k % 2, lambda: step_sum(k))
    total = jnp.sum(jnp.sum(tiles[-1], axis=0, keepdims=True), axis=1, keepdims=True)
    mean = total * (COUPLING / TOTAL_CELLS)
    work_ref[...] = work_ref[...] + mean * (4.0 / 6.0)
    dens_ref[...] = dens_ref[...] - mean

    def later(k, carry):
        sweep(lax.rem(k, 2), lambda: None)
        return carry

    lax.fori_loop(4, 8, later, 0)

    for copy in deposits:
        copy.wait_send()
    phi = work_ref[...]
    high, layers, copies = exchange_start(phi, 0)
    phi_copy = send(work_ref, phi_got, one_ss.at[3], one_rs.at[3], owner)
    sign = jnp.where(iota((1, 128), 1) < S, 0.5, -0.5).astype(bf16)
    raw = home_ghosts(phi, high, layers)
    local = []
    for d in range(3):
        up, down = inner(phi, d)
        part = placed(raw, d, sign)
        local.append(0.5 * (down - up) + part[0:O] + part[O : 2 * O])
    for copy in copies:
        copy.wait_recv()
    raw = away_ghosts(0)
    field = [(local[d] + placed(raw, d, sign)).astype(bf16) for d in range(3)]
    fhome_send[...] = jnp.concatenate(field, axis=0)
    fhome_copy = send(fhome_send, fhome_got, one_ss.at[2], one_rs.at[2], owner)
    row_dim = iota((ROWS, 1), 0) % 16 // 4
    picked = [dot(slot_octs, field[d]) for d in range(3)]
    msg_send[...] = jnp.where(
        row_dim == 0, picked[0], jnp.where(row_dim == 1, picked[1], picked[2])
    ).astype(bf16)
    returns = send_lanes(msg_send, field_got, msg_ss, field_rs, holders)
    phi_copy.wait_recv()
    phi_ref[...] = phi_got[...]
    fhome_copy.wait_recv()
    for copy in returns:
        copy.wait_recv()
    got = field_got[...]
    for d in range(3):
        values = dot(at_home[:, 0:O], fhome_got[O * d : O * d + O]) + dot(into[d], got)
        for i in range(4):
            pair = values[:, 128 * i : 128 * i + 128]
            turned = pltpu.roll(pair, S, 1)
            field_ref[d, pl.ds(2 * i, B, stride=8), :] = jnp.where(low_half, pair, turned)
            field_ref[d, pl.ds(2 * i + 1, B, stride=8), :] = jnp.where(low_half, turned, pair)

    def interpolate(i, carry):
        rows = pl.ds(pl.multiple_of(i * 8, 8), 8)
        xs, ys, zs = pos_ref[0, rows, :], pos_ref[1, rows, :], pos_ref[2, rows, :]
        out = [[], [], []]
        for r in range(8):
            wx = weights(xs[r : r + 1])
            high, low = crossed(weights(ys[r : r + 1]), weights(zs[r : r + 1]))
            at = pl.ds(pl.multiple_of(i * 64 + 8 * r, 8), 8)
            left = jnp.concatenate([field_ref[d, at, :] for d in range(3)], axis=0).astype(bf16)
            value = dot(left, jnp.concatenate([high, low], axis=0))
            for d in range(3):
                out[d].append(jnp.sum(value[8 * d : 8 * d + 8] * wx, axis=0, keepdims=True))
        for d in range(3):
            accel_ref[d, rows, :] = jnp.concatenate(out[d], axis=0)
        return carry

    lax.fori_loop(0, B // 8, interpolate, 0)

    for copy in [index_copy, home_copy, phi_copy, fhome_copy] + requests + sums + copies + returns:
        copy.wait_send()


def on_device(
    positions, masses, block_owner, block_oct, face_owner, face_oct, face_coarse, face_quadrant
):
    dma = pltpu.SemaphoreType.DMA
    vmem = pl.BlockSpec(memory_space=pltpu.VMEM)
    potential, accel = pl.pallas_call(
        kernel,
        out_shape=(
            jax.ShapeDtypeStruct((O, C), f32),
            jax.ShapeDtypeStruct((3, B, PART), f32),
        ),
        in_specs=[vmem] * 8,
        out_specs=(vmem, vmem),
        scratch_shapes=[
            pltpu.VMEM((B * 8, 128), f32),
            pltpu.VMEM((ROWS, 256), bf16),
            pltpu.VMEM((ROWS, 256), bf16),
            pltpu.VMEM((ROWS, C), bf16),
            pltpu.VMEM((ROWS, C), bf16),
            pltpu.VMEM((ROWS, C), bf16),
            pltpu.VMEM((ROWS, 128), bf16),
            pltpu.VMEM((2, ROWS, 128), bf16),
            pltpu.VMEM((4, 8, 128), f32),
            pltpu.VMEM((10, 8, 128), f32),
            pltpu.VMEM((3, B * 8, 128), f32),
            pltpu.VMEM((O, C), f32),
            pltpu.VMEM((2 * O, F6), bf16),
            pltpu.VMEM((2 * O, F6), bf16),
            pltpu.VMEM((O, F6), bf16),
            pltpu.VMEM((ROWS, F6), f32),
            pltpu.VMEM((ROWS, F6), bf16),
            pltpu.VMEM((O, ROWS), bf16),
            pltpu.VMEM((ROWS, S), bf16),
            pltpu.VMEM((C, F6), bf16),
            pltpu.VMEM((768, C), bf16),
            pltpu.VMEM((F6, F6), bf16),
            pltpu.VMEM((128, 128), f32),
            pltpu.VMEM((32, 128), f32),
            pltpu.VMEM((O, C), f32),
            pltpu.VMEM((O, C), f32),
            pltpu.VMEM((3 * O, C), bf16),
            pltpu.VMEM((3 * O, C), bf16),
            pltpu.VMEM((O, C), f32),
            pltpu.VMEM((O, C), f32),
            dma((LANES,)),
            dma((LANES,)),
            dma((LANES,)),
            dma((LANES,)),
            dma((LANES,)),
            dma((LANES,)),
            dma((2, LANES)),
            dma((10,)),
            dma((10,)),
            dma((4,)),
            dma((4,)),
        ],
        compiler_params=pltpu.CompilerParams(
            collective_id=0, has_side_effects=True, vmem_limit_bytes=40 * 1024 * 1024
        ),
    )(
        jnp.transpose(positions, (1, 0, 2)),
        masses,
        block_owner.T,
        block_oct[None, :],
        jnp.transpose(face_owner, (1, 2, 0)),
        face_oct.T,
        face_coarse.T,
        face_quadrant.T,
    )
    return potential, jnp.transpose(accel, (1, 0, 2))


def solution(mesh):
    placed = (
        P("hilbert", None, None),
        P("hilbert", None),
        P("hilbert", None),
        P("hilbert"),
        P("hilbert", None, None),
        P("hilbert", None),
        P("hilbert", None),
        P("hilbert", None),
    )
    return jax.shard_map(
        on_device,
        mesh=mesh,
        in_specs=placed,
        out_specs=(P("hilbert", None), P("hilbert", None, None)),
        check_vma=False,
    )
```

```python
import jax
import jax.numpy as jnp
from jax import lax
from jax.experimental import pallas as pl
from jax.experimental.pallas import tpu as pltpu
from jax.sharding import PartitionSpec as P

N = 128
B = 128
O = 64
C = 512
S = 64
F6 = 6 * S
PART = 256
OFFS = (1, 2, 3, 4, 127, 126, 125, 124, 64)
BACK = (4, 5, 6, 7, 0, 1, 2, 3, 8)
LANES = len(OFFS)
LANE_ORDER = (8, 3, 7, 2, 6, 1, 5, 0, 4)
ROWS = 16 * LANES
TOTAL_CELLS = float(N * O * C)
COUPLING = 0.25

f32 = jnp.float32
bf16 = jnp.bfloat16
i32 = jnp.int32


def dot(a, b):
    return jnp.dot(a, b, preferred_element_type=f32)


def dot_t(a, b):
    return lax.dot_general(a, b, (((0,), (0,)), ((), ())), preferred_element_type=f32)


def iota(shape, dim):
    return lax.broadcasted_iota(i32, shape, dim)


def pick_table(d):
    cell, lane = iota((C, 128), 0), iota((C, 128), 1)
    coord, spot = cell_spot(cell, d)
    return ((coord == jnp.where(lane < S, 7, 0)) & (spot == lane % S)).astype(f32).astype(bf16)


def place_table(d):
    row, cell = iota((256, C), 0), iota((256, C), 1)
    coord, spot = cell_spot(cell, d)
    j = row % S
    here = coord == (row // S % 2) * 7
    fine = spot == j
    coarse = ((spot // 16) == (j // 8 % 4)) & ((spot % 8) // 2 == j % 4)
    return (here & (((row < 128) & fine) | ((row >= 128) & coarse))).astype(f32).astype(bf16)


def cell_spot(cell, d):
    x, y, z = cell // 64, cell // 8 % 8, cell % 8
    return ((x, y * 8 + z), (y, x * 8 + z), (z, x * 8 + y))[d]


def weights(row):
    centres = iota((8, PART), 0).astype(f32) + 0.5
    return jnp.maximum(0.0, 1.0 - jnp.abs(row - centres))


def crossed(wy, wz):
    full = jnp.concatenate([wy[y : y + 1] * wz for y in range(8)], axis=0)
    high = full.astype(bf16)
    return high, (full - high.astype(f32)).astype(bf16)


def device_at(x, z, y, core):
    return x * 32 + z * 8 + y * 2 + core


def host_of(i):
    x, z, y = i // 32, lax.rem(i // 8, 4), lax.rem(i // 2, 4)
    return device_at(
        lax.rem(x + 3, 4),
        z + lax.rem(x, 2) * (3 - 2 * z),
        y + lax.rem(z, 2) * (3 - 2 * y),
        lax.rem(i, 2),
    )


def hosted_by(i):
    x, z, y = lax.rem(i // 32 + 1, 4), lax.rem(i // 8, 4), lax.rem(i // 2, 4)
    z = z + lax.rem(x, 2) * (3 - 2 * z)
    return device_at(x, z, y + lax.rem(z, 2) * (3 - 2 * y), lax.rem(i, 2))


def kernel(
    pos_hbm, mass_hbm, bown_ref, boct_ref, fown_ref, foct_ref, fco_ref, fq_ref,
    phi_ref, accel_ref,
    dep_ref, req_send, req_got, msg_send, dep_got, field_got, face_send, face_got,
    sum_send, sum_got, field_ref, dens_ref, m0_ref, mc_ref, home_ref, fmask_ref, smask_ref, gro_ref, os_ref,
    pick_ref, place_ref, diag_ref, index_ref, index_got, home_send, home_got, fhome_send, fhome_got,
    work_ref, phi_got, pos_ref, mass_ref, cross_ref, homelo_send, homelo_got,
    req_ss, req_rs, msg_ss, dep_rs, field_rs, face_ss, face_rs, sum_ss, sum_rs, one_ss, one_rs, load_sem,
):
    me = lax.axis_index("hilbert")
    owner = hosted_by(me)
    my_host = host_of(me)
    near = [lax.rem(me + o, N) for o in OFFS]
    hosts = [host_of(p) for p in near]
    holders = [lax.rem(owner + o, N) for o in OFFS]
    peers = [host_of(p) for p in holders]
    stages = []
    for stride, size in ((1, 2), (2, 4), (8, 4), (32, 4)):
        digit = lax.rem(me // stride, size)
        stages.append(
            [(me + (lax.rem(digit + j, size) - digit) * stride, size - 1 - j) for j in range(1, size)]
        )
    first_sum = (0, 1, 4, 7)

    barrier = pltpu.get_barrier_semaphore()
    partners = peers + hosts + holders + [my_host, owner] + [p for stage in stages for p, _ in stage]
    for p in partners:
        pl.semaphore_signal(barrier, inc=1, device_id=(p,), device_id_type=pl.DeviceIdType.MESH)

    loads = [
        pltpu.make_async_copy(mass_hbm, mass_ref, load_sem.at[0]),
        pltpu.make_async_copy(pos_hbm, pos_ref, load_sem.at[1]),
    ]
    for copy in loads:
        copy.start()

    def send(src, dst, ss, rs, p):
        copy = pltpu.make_async_remote_copy(
            src_ref=src, dst_ref=dst, send_sem=ss, recv_sem=rs,
            device_id=(p,), device_id_type=pl.DeviceIdType.MESH,
        )
        copy.start()
        return copy

    def send_lanes(src, dst, ss, rs, to):
        return [
            send(
                src.at[pl.ds(16 * l, 16)], dst.at[pl.ds(16 * BACK[l], 16)],
                ss.at[l], rs.at[BACK[l]], to[l],
            )
            for l in LANE_ORDER
        ]

    lane128 = iota((1, 128), 1)
    offs_row = jnp.where(
        lane128 < 4,
        lane128 + 1,
        jnp.where(lane128 < 8, 131 - lane128, jnp.where(lane128 == 8, 64, -1)),
    )
    lane_f = lane128.astype(f32)

    def slots_of(match):
        rows = match.shape[0]
        earlier = (iota((rows, rows), 0) > iota((rows, rows), 1)).astype(f32).astype(bf16)
        rank = jnp.sum(dot(earlier, match.astype(bf16)) * match, axis=1, keepdims=True)
        lane = jnp.sum(match * lane_f, axis=1, keepdims=True)
        away = jnp.sum(match, axis=1, keepdims=True)
        return jnp.where(away > 0.5, lane * 16.0 + rank, -1000.0)

    def face_slots(columns, of):
        delta = (columns[0:O, 0:6] - of + N) % N
        match = jnp.concatenate(
            [(delta[:, f : f + 1] == offs_row).astype(f32) for f in range(6)], axis=0
        )
        return (slots_of(match) == iota((F6, ROWS), 1).astype(f32)).astype(f32)

    index_ref[...] = jnp.zeros((128, 128), f32)
    for f in range(6):
        index_ref[f : f + 1, 0:O] = fown_ref[f].astype(f32)
        index_ref[8 + f : 9 + f, 0:O] = foct_ref[f : f + 1].astype(f32)
        index_ref[16 + f : 17 + f, 0:O] = fco_ref[f : f + 1].astype(f32)
        index_ref[24 + f : 25 + f, 0:O] = fq_ref[f : f + 1].astype(f32)
    index_ref[32:33, :] = bown_ref[...].astype(f32)
    index_ref[33:34, :] = boct_ref[...].astype(f32)
    columns = index_ref[...].T.astype(i32)

    takes = face_slots(columns, me)
    oct_col = jnp.concatenate([columns[0:O, 8 + f : 9 + f] for f in range(6)], axis=0)
    lane_wide = iota((F6, 128), 1)
    row_face = iota((F6, 128), 0) // O
    wanted = jnp.where(
        lane_wide < S, (oct_col == lane_wide).astype(f32), (lane_wide - S == row_face).astype(f32)
    ).astype(bf16)

    block_delta = (columns[:, 32:33] - me + N) % N
    block_slot = slots_of((block_delta == offs_row).astype(f32))
    slot_lane = iota((B, ROWS), 1).astype(f32)
    into = [(block_slot + 4.0 * d == slot_lane).astype(f32).astype(bf16) for d in range(3)]
    oct_is = columns[:, 33:34] == iota((B, 128), 1)
    at_home = ((block_delta == 0) & oct_is).astype(f32).astype(bf16)
    oct_hot = oct_is.astype(f32).astype(bf16)
    req_send[:, 0:128] = dot_t(takes.astype(bf16), wanted).astype(bf16)
    req_send[:, 128:256] = dot_t(into[0] + into[1] + into[2], oct_hot).astype(bf16)

    for copy in loads:
        copy.wait()
    masses = mass_ref[...]
    tile = masses[0:8, 0:128]
    for r in range(16):
        for h in range(2):
            if r or h:
                tile = tile + masses[8 * r : 8 * r + 8, 128 * h : 128 * h + 128]

    def deposit(i, carry):
        rows = pl.ds(pl.multiple_of(i * 8, 8), 8)
        xs, ys, zs, ms = pos_ref[0, rows, :], pos_ref[1, rows, :], pos_ref[2, rows, :], mass_ref[rows, :]
        for r in range(8):
            wx = weights(xs[r : r + 1]) * ms[r : r + 1]
            high, low = crossed(weights(ys[r : r + 1]), weights(zs[r : r + 1]))
            x_high = wx.astype(bf16).astype(f32)
            left = jnp.concatenate([x_high, wx - x_high], axis=0).astype(bf16)
            right = jnp.concatenate([high, low], axis=0)
            both = lax.dot_general(
                left, right, (((1,), (1,)), ((), ())), preferred_element_type=f32
            )
            dep_ref[pl.ds(pl.multiple_of(i * 64 + 8 * r, 8), 8), :] = both[0:8] + both[8:16]
            cross_ref[pl.ds(pl.multiple_of(i * 1024 + 128 * r, 128), 128), :] = right
        return carry

    lax.fori_loop(0, B // 16, deposit, 0)

    pl.semaphore_wait(barrier, len(partners))

    requests = send_lanes(req_send, req_got, req_ss, req_rs, hosts)
    index_copy = send(index_ref.at[pl.ds(0, 32)], index_got, one_ss.at[0], one_rs.at[0], my_host)
    sums = []

    def sum_start(s, tile):
        sum_send[s] = tile
        for j, (p, back) in enumerate(stages[s]):
            at = first_sum[s]
            sums.append(
                send(sum_send.at[s], sum_got.at[at + back], sum_ss.at[at + j], sum_rs.at[at + back], p)
            )

    def sum_end(s, tile):
        at, count = first_sum[s], len(stages[s])
        for copy in sums[at : at + count]:
            copy.wait_recv()
        for j in range(count):
            tile = tile + sum_got[at + j]
        return tile

    sum_start(0, tile)

    lax.fori_loop(B // 16, B // 8, deposit, 0)

    low_half = iota((B, 128), 1) < S
    parts = []
    for i in range(4):
        even = dep_ref[pl.ds(2 * i, B, stride=8), :]
        odd = dep_ref[pl.ds(2 * i + 1, B, stride=8), :]
        parts.append(
            jnp.where(low_half, even + pltpu.roll(even, S, 1), odd + pltpu.roll(odd, S, 1))
        )
    rest = jnp.concatenate(parts, axis=1)
    pieces = []
    for _ in range(3):
        piece = rest.astype(bf16)
        rest = rest - piece.astype(f32)
        pieces.append(piece)
    stacked = jnp.concatenate(pieces, axis=0)
    msg_send[...] = dot_t(jnp.concatenate(into, axis=0), stacked).astype(bf16)
    deposits = send_lanes(msg_send, dep_got, msg_ss, dep_rs, hosts)
    home = dot_t(jnp.concatenate([at_home] * 3, axis=0), stacked)[0:O]
    home_send[...] = home.astype(bf16)
    home_copy = send(home_send, home_got, one_ss.at[1], one_rs.at[1], my_host)
    homelo_send[...] = (home - home.astype(bf16).astype(f32)).astype(bf16)
    homelo_copy = send(homelo_send, homelo_got, one_ss.at[4], one_rs.at[4], my_host)

    for d in range(3):
        pick_ref[:, 128 * d : 128 * d + 128] = pick_table(d)
        place_ref[256 * d : 256 * d + 256, :] = place_table(d)
    diag_ref[...] = (iota((F6, F6), 0) // S == iota((F6, F6), 1) // S).astype(f32).astype(bf16)
    to_face = (iota((128, F6), 0) - S == iota((128, F6), 1) // S).astype(f32).astype(bf16)

    tile = sum_end(0, tile)
    sum_start(1, tile)

    index_copy.wait_recv()
    spare = jnp.zeros((96, 128), f32)
    columns = jnp.concatenate([index_got[...], spare], axis=0).T.astype(i32)
    group = iota((O, F6), 1) // S

    def spread(base):
        total = jnp.zeros((O, F6), i32)
        for f in range(6):
            total = jnp.where(group == f, columns[0:O, base + f : base + f + 1], total)
        return total

    takes = face_slots(columns, owner)
    gro = takes[0:O]
    for f in range(1, 6):
        gro = gro + takes[f * O : (f + 1) * O]
    gro_ref[...] = gro.astype(bf16)
    same_face = (iota((F6, F6), 0) // O == iota((F6, F6), 1) // S).astype(f32).astype(bf16)
    smask_ref[...] = dot_t(takes.astype(bf16), same_face).astype(bf16)
    inside = iota((O, F6), 1) % S
    home_ref[...] = ((spread(0) == owner) & (spread(8) == inside)).astype(f32).astype(bf16)
    coarse_x = spread(16)
    quad_x = spread(24)
    quad_in = (inside // 32) * 2 + (inside % 8) // 4
    m0 = (coarse_x != 1).astype(f32).astype(bf16)
    mc = ((coarse_x == 1) & (quad_x == quad_in)).astype(f32).astype(bf16)
    m0_ref[...] = jnp.concatenate([m0, m0], axis=0)
    mc_ref[...] = jnp.concatenate([mc, mc], axis=0)

    for copy in requests:
        copy.wait_recv()
    asks = req_got[...]
    os_ref[...] = asks[:, 0:S]
    fmask_ref[...] = dot(asks[:, 0:128], to_face)
    slot_octs = asks[:, 128 : 128 + S]

    for copy in deposits:
        copy.wait_recv()
    density = dot_t(slot_octs, dep_got[...])
    home_copy.wait_recv()
    source = COUPLING * (density + home_got[...].astype(f32))
    dens_ref[...] = source
    work_ref[...] = source * (-1.0 / 6.0)

    lane = iota((1, C), 1)
    at = (lane // 64, lane // 8 % 8, lane % 8)
    strides = (64, 8, 1)

    def inner(phi, d):
        up = jnp.where(at[d] < 7, pltpu.roll(phi, C - strides[d], 1), 0.0)
        down = jnp.where(at[d] > 0, pltpu.roll(phi, strides[d], 1), 0.0)
        return up, down

    def placed(raw, d, sign):
        rows = raw.shape[0]
        part = raw[:, 128 * d : 128 * d + 128]
        if sign is not None:
            part = part * sign
        left = jnp.concatenate(
            [part * m0_ref[0:rows, 128 * d : 128 * d + 128], part * mc_ref[0:rows, 128 * d : 128 * d + 128]],
            axis=1,
        )
        return dot(left, place_ref[256 * d : 256 * d + 256, :])

    def exchange_start(phi, slot):
        high = phi.astype(bf16)
        layers = dot(high, pick_ref[...]).astype(bf16)
        chosen = dot(os_ref[...], layers) * fmask_ref[...]
        out = chosen[:, 0:128] + chosen[:, 128:256] + chosen[:, 256:384]
        face_send[...] = (out + pltpu.roll(out, S, 1)).astype(bf16)
        copies = send_lanes(face_send, face_got.at[slot], face_ss, face_rs.at[slot], peers)
        return high, layers, copies

    def home_ghosts(phi, high, layers):
        low = (phi - high.astype(f32)).astype(bf16)
        layers_low = dot(low, pick_ref[...]).astype(bf16)
        diag = diag_ref[...]
        wide = [jnp.concatenate([x] * 6, axis=0) * diag for x in (layers, layers_low)]
        return jnp.concatenate([dot(home_ref[...], x).astype(bf16) for x in wide], axis=0)

    def away_ghosts(slot):
        got = face_got[slot]
        return dot(gro_ref[...], jnp.concatenate([got] * 3, axis=1) * smask_ref[...]).astype(bf16)

    def sweep(slot, between):
        high, layers, copies = exchange_start(work_ref[...], slot)
        between()
        phi = work_ref[...]
        raw = home_ghosts(phi, high, layers)
        total = placed(raw, 0, None) + placed(raw, 1, None) + placed(raw, 2, None)
        total = total[0:O] + total[O : 2 * O] - dens_ref[...]
        for d in range(3):
            up, down = inner(phi, d)
            total = total + (up + down)
        for copy in copies:
            copy.wait_recv()
        raw = away_ghosts(slot)
        total = total + (placed(raw, 0, None) + placed(raw, 1, None) + placed(raw, 2, None))
        work_ref[...] = total * (1.0 / 6.0)
        for copy in copies:
            copy.wait_send()

    tiles = [tile]

    def step_sum(s):
        tiles.append(sum_end(s, tiles[-1]))
        if s < 3:
            sum_start(s + 1, tiles[-1])

    def add_low():
        homelo_copy.wait_recv()
        low = COUPLING * homelo_got[...].astype(f32)
        dens_ref[...] = dens_ref[...] + low
        work_ref[...] = work_ref[...] - low * (1.0 / 6.0)
        step_sum(1)

    sweep(1, add_low)
    sweep(0, lambda: step_sum(2))
    sweep(1, lambda: step_sum(3))
    total = jnp.sum(jnp.sum(tiles[-1], axis=0, keepdims=True), axis=1, keepdims=True)
    mean = total * (COUPLING / TOTAL_CELLS)
    work_ref[...] = work_ref[...] + mean * (4.0 / 6.0)
    dens_ref[...] = dens_ref[...] - mean

    def later(k, carry):
        sweep(lax.rem(k, 2), lambda: None)
        return carry

    lax.fori_loop(4, 8, later, 0)

    for copy in deposits:
        copy.wait_send()
    phi = work_ref[...]
    high, layers, copies = exchange_start(phi, 0)
    phi_copy = send(work_ref, phi_got, one_ss.at[3], one_rs.at[3], owner)
    sign = jnp.where(iota((1, 128), 1) < S, 0.5, -0.5).astype(bf16)
    raw = home_ghosts(phi, high, layers)
    local = []
    for d in range(3):
        up, down = inner(phi, d)
        part = placed(raw, d, sign)
        local.append(0.5 * (down - up) + part[0:O] + part[O : 2 * O])
    for copy in copies:
        copy.wait_recv()
    raw = away_ghosts(0)
    field = [(local[d] + placed(raw, d, sign)).astype(bf16) for d in range(3)]
    fhome_send[...] = jnp.concatenate(field, axis=0)
    fhome_copy = send(fhome_send, fhome_got, one_ss.at[2], one_rs.at[2], owner)
    row_dim = iota((ROWS, 1), 0) % 16 // 4
    picked = [dot(slot_octs, field[d]) for d in range(3)]
    msg_send[...] = jnp.where(
        row_dim == 0, picked[0], jnp.where(row_dim == 1, picked[1], picked[2])
    ).astype(bf16)
    returns = send_lanes(msg_send, field_got, msg_ss, field_rs, holders)
    phi_copy.wait_recv()
    phi_ref[...] = phi_got[...]
    fhome_copy.wait_recv()
    for copy in returns:
        copy.wait_recv()
    got = field_got[...]
    for d in range(3):
        values = dot(at_home[:, 0:O], fhome_got[O * d : O * d + O]) + dot(into[d], got)
        for i in range(4):
            pair = values[:, 128 * i : 128 * i + 128]
            turned = pltpu.roll(pair, S, 1)
            field_ref[d, pl.ds(2 * i, B, stride=8), :] = jnp.where(low_half, pair, turned)
            field_ref[d, pl.ds(2 * i + 1, B, stride=8), :] = jnp.where(low_half, turned, pair)

    def interpolate(i, carry):
        rows = pl.ds(pl.multiple_of(i * 8, 8), 8)
        xs = pos_ref[0, rows, :]
        out = [[], [], []]
        for r in range(8):
            wx = weights(xs[r : r + 1])
            both = cross_ref[pl.ds(pl.multiple_of(i * 1024 + 128 * r, 128), 128), :]
            at = pl.ds(pl.multiple_of(i * 64 + 8 * r, 8), 8)
            left = jnp.concatenate([field_ref[d, at, :] for d in range(3)], axis=0).astype(bf16)
            value = dot(left, both)
            for d in range(3):
                out[d].append(jnp.sum(value[8 * d : 8 * d + 8] * wx, axis=0, keepdims=True))
        for d in range(3):
            accel_ref[d, rows, :] = jnp.concatenate(out[d], axis=0)
        return carry

    lax.fori_loop(0, B // 8, interpolate, 0)

    for copy in [index_copy, home_copy, homelo_copy, phi_copy, fhome_copy] + requests + sums + copies + returns:
        copy.wait_send()


def on_device(
    positions, masses, block_owner, block_oct, face_owner, face_oct, face_coarse, face_quadrant
):
    dma = pltpu.SemaphoreType.DMA
    vmem = pl.BlockSpec(memory_space=pltpu.VMEM)
    potential, accel = pl.pallas_call(
        kernel,
        out_shape=(
            jax.ShapeDtypeStruct((O, C), f32),
            jax.ShapeDtypeStruct((3, B, PART), f32),
        ),
        in_specs=[pl.BlockSpec(memory_space=pl.ANY)] * 2 + [vmem] * 6,
        out_specs=(vmem, vmem),
        scratch_shapes=[
            pltpu.VMEM((B * 8, 128), f32),
            pltpu.VMEM((ROWS, 256), bf16),
            pltpu.VMEM((ROWS, 256), bf16),
            pltpu.VMEM((ROWS, C), bf16),
            pltpu.VMEM((ROWS, C), bf16),
            pltpu.VMEM((ROWS, C), bf16),
            pltpu.VMEM((ROWS, 128), bf16),
            pltpu.VMEM((2, ROWS, 128), bf16),
            pltpu.VMEM((4, 8, 128), f32),
            pltpu.VMEM((10, 8, 128), f32),
            pltpu.VMEM((3, B * 8, 128), f32),
            pltpu.VMEM((O, C), f32),
            pltpu.VMEM((2 * O, F6), bf16),
            pltpu.VMEM((2 * O, F6), bf16),
            pltpu.VMEM((O, F6), bf16),
            pltpu.VMEM((ROWS, F6), f32),
            pltpu.VMEM((ROWS, F6), bf16),
            pltpu.VMEM((O, ROWS), bf16),
            pltpu.VMEM((ROWS, S), bf16),
            pltpu.VMEM((C, F6), bf16),
            pltpu.VMEM((768, C), bf16),
            pltpu.VMEM((F6, F6), bf16),
            pltpu.VMEM((128, 128), f32),
            pltpu.VMEM((32, 128), f32),
            pltpu.VMEM((O, C), bf16),
            pltpu.VMEM((O, C), bf16),
            pltpu.VMEM((3 * O, C), bf16),
            pltpu.VMEM((3 * O, C), bf16),
            pltpu.VMEM((O, C), f32),
            pltpu.VMEM((O, C), f32),
            pltpu.VMEM((3, B, PART), f32),
            pltpu.VMEM((B, PART), f32),
            pltpu.VMEM((B * 128, PART), bf16),
            pltpu.VMEM((O, C), bf16),
            pltpu.VMEM((O, C), bf16),
            dma((LANES,)),
            dma((LANES,)),
            dma((LANES,)),
            dma((LANES,)),
            dma((LANES,)),
            dma((LANES,)),
            dma((2, LANES)),
            dma((10,)),
            dma((10,)),
            dma((5,)),
            dma((5,)),
            dma((2,)),
        ],
        compiler_params=pltpu.CompilerParams(
            collective_id=0, has_side_effects=True, vmem_limit_bytes=40 * 1024 * 1024
        ),
    )(
        jnp.transpose(positions, (1, 0, 2)),
        masses,
        block_owner.T,
        block_oct[None, :],
        jnp.transpose(face_owner, (1, 2, 0)),
        face_oct.T,
        face_coarse.T,
        face_quadrant.T,
    )
    return potential, jnp.transpose(accel, (1, 0, 2))


def solution(mesh):
    placed = (
        P("hilbert", None, None),
        P("hilbert", None),
        P("hilbert", None),
        P("hilbert"),
        P("hilbert", None, None),
        P("hilbert", None),
        P("hilbert", None),
        P("hilbert", None),
    )
    return jax.shard_map(
        on_device,
        mesh=mesh,
        in_specs=placed,
        out_specs=(P("hilbert", None), P("hilbert", None, None)),
        check_vma=False,
    )
```

```python
import jax
import jax.numpy as jnp
from jax import lax
from jax.experimental import pallas as pl
from jax.experimental.pallas import tpu as pltpu
from jax.sharding import PartitionSpec as P

N = 128
B = 128
O = 64
C = 512
S = 64
F6 = 6 * S
PART = 256
OFFS = (1, 2, 3, 4, 127, 126, 125, 124, 64)
BACK = (4, 5, 6, 7, 0, 1, 2, 3, 8)
LANES = len(OFFS)
LANE_ORDER = (8, 3, 7, 2, 6, 1, 5, 0, 4)
ROWS = 16 * LANES
TOTAL_CELLS = float(N * O * C)
COUPLING = 0.25

f32 = jnp.float32
bf16 = jnp.bfloat16
i32 = jnp.int32


def dot(a, b):
    return jnp.dot(a, b, preferred_element_type=f32)


def dot_t(a, b):
    return lax.dot_general(a, b, (((0,), (0,)), ((), ())), preferred_element_type=f32)


def iota(shape, dim):
    return lax.broadcasted_iota(i32, shape, dim)


def pick_table(d):
    cell, lane = iota((C, 128), 0), iota((C, 128), 1)
    coord, spot = cell_spot(cell, d)
    return ((coord == jnp.where(lane < S, 7, 0)) & (spot == lane % S)).astype(f32).astype(bf16)


def place_table(d):
    row, cell = iota((256, C), 0), iota((256, C), 1)
    coord, spot = cell_spot(cell, d)
    j = row % S
    here = coord == (row // S % 2) * 7
    fine = spot == j
    coarse = ((spot // 16) == (j // 8 % 4)) & ((spot % 8) // 2 == j % 4)
    return (here & (((row < 128) & fine) | ((row >= 128) & coarse))).astype(f32).astype(bf16)


def cell_spot(cell, d):
    x, y, z = cell // 64, cell // 8 % 8, cell % 8
    return ((x, y * 8 + z), (y, x * 8 + z), (z, x * 8 + y))[d]


def weights(row):
    centres = iota((8, PART), 0).astype(f32) + 0.5
    return jnp.maximum(0.0, 1.0 - jnp.abs(row - centres))


def crossed(wy, wz):
    full = jnp.concatenate([wy[y : y + 1] * wz for y in range(8)], axis=0)
    high = full.astype(bf16)
    return high, (full - high.astype(f32)).astype(bf16)


def device_at(x, z, y, core):
    return x * 32 + z * 8 + y * 2 + core


def host_of(i):
    x, z, y = i // 32, lax.rem(i // 8, 4), lax.rem(i // 2, 4)
    return device_at(
        lax.rem(x + 3, 4),
        z + lax.rem(x, 2) * (3 - 2 * z),
        y + lax.rem(z, 2) * (3 - 2 * y),
        lax.rem(i, 2),
    )


def hosted_by(i):
    x, z, y = lax.rem(i // 32 + 1, 4), lax.rem(i // 8, 4), lax.rem(i // 2, 4)
    z = z + lax.rem(x, 2) * (3 - 2 * z)
    return device_at(x, z, y + lax.rem(z, 2) * (3 - 2 * y), lax.rem(i, 2))


def kernel(
    pos_hbm, mass_hbm, bown_ref, boct_ref, fown_ref, foct_ref, fco_ref, fq_ref,
    phi_ref, accel_ref,
    dep_ref, req_send, req_got, msg_send, dep_got, field_got, face_send, face_got,
    sum_send, sum_got, field_ref, dens_ref, m0_ref, mc_ref, home_ref, fmask_ref, smask_ref, gro_ref, os_ref,
    pick_ref, place_ref, diag_ref, index_ref, index_got, home_send, home_got, layers_got,
    work_ref, phi_got, pos_ref, mass_ref, cross_ref, homelo_send, homelo_got,
    req_ss, req_rs, msg_ss, dep_rs, field_rs, face_ss, face_rs, sum_ss, sum_rs, one_ss, one_rs, load_sem,
):
    me = lax.axis_index("hilbert")
    owner = hosted_by(me)
    my_host = host_of(me)
    near = [lax.rem(me + o, N) for o in OFFS]
    hosts = [host_of(p) for p in near]
    holders = [lax.rem(owner + o, N) for o in OFFS]
    peers = [host_of(p) for p in holders]
    stages = []
    for stride, size in ((1, 2), (2, 4), (8, 4), (32, 4)):
        digit = lax.rem(me // stride, size)
        stages.append(
            [(me + (lax.rem(digit + j, size) - digit) * stride, size - 1 - j) for j in range(1, size)]
        )
    first_sum = (0, 1, 4, 7)

    barrier = pltpu.get_barrier_semaphore()
    partners = peers + hosts + holders + [my_host, owner] + [p for stage in stages for p, _ in stage]
    for p in partners:
        pl.semaphore_signal(barrier, inc=1, device_id=(p,), device_id_type=pl.DeviceIdType.MESH)

    loads = [
        pltpu.make_async_copy(mass_hbm, mass_ref, load_sem.at[0]),
        pltpu.make_async_copy(pos_hbm, pos_ref, load_sem.at[1]),
    ]
    for copy in loads:
        copy.start()

    def send(src, dst, ss, rs, p):
        copy = pltpu.make_async_remote_copy(
            src_ref=src, dst_ref=dst, send_sem=ss, recv_sem=rs,
            device_id=(p,), device_id_type=pl.DeviceIdType.MESH,
        )
        copy.start()
        return copy

    def send_lanes(src, dst, ss, rs, to):
        return [
            send(
                src.at[pl.ds(16 * l, 16)], dst.at[pl.ds(16 * BACK[l], 16)],
                ss.at[l], rs.at[BACK[l]], to[l],
            )
            for l in LANE_ORDER
        ]

    lane128 = iota((1, 128), 1)
    offs_row = jnp.where(
        lane128 < 4,
        lane128 + 1,
        jnp.where(lane128 < 8, 131 - lane128, jnp.where(lane128 == 8, 64, -1)),
    )
    lane_f = lane128.astype(f32)

    def slots_of(match):
        rows = match.shape[0]
        earlier = (iota((rows, rows), 0) > iota((rows, rows), 1)).astype(f32).astype(bf16)
        rank = jnp.sum(dot(earlier, match.astype(bf16)) * match, axis=1, keepdims=True)
        lane = jnp.sum(match * lane_f, axis=1, keepdims=True)
        away = jnp.sum(match, axis=1, keepdims=True)
        return jnp.where(away > 0.5, lane * 16.0 + rank, -1000.0)

    def face_slots(columns, of):
        delta = (columns[0:O, 0:6] - of + N) % N
        match = jnp.concatenate(
            [(delta[:, f : f + 1] == offs_row).astype(f32) for f in range(6)], axis=0
        )
        return (slots_of(match) == iota((F6, ROWS), 1).astype(f32)).astype(f32)

    def set_tables(role, columns, of):
        group = iota((O, F6), 1) // S
        inside = iota((O, F6), 1) % S

        def spread(base):
            total = jnp.zeros((O, F6), i32)
            for f in range(6):
                total = jnp.where(group == f, columns[0:O, base + f : base + f + 1], total)
            return total

        takes = face_slots(columns, of)
        gro = takes[0:O]
        for f in range(1, 6):
            gro = gro + takes[f * O : (f + 1) * O]
        gro_ref[role] = gro.astype(bf16)
        same_face = (iota((F6, F6), 0) // O == iota((F6, F6), 1) // S).astype(f32).astype(bf16)
        smask_ref[role] = dot_t(takes.astype(bf16), same_face).astype(bf16)
        home_ref[role] = ((spread(0) == of) & (spread(8) == inside)).astype(f32).astype(bf16)
        coarse_x = spread(16)
        quad_x = spread(24)
        quad_in = (inside // 32) * 2 + (inside % 8) // 4
        m0 = (coarse_x != 1).astype(f32).astype(bf16)
        mc = ((coarse_x == 1) & (quad_x == quad_in)).astype(f32).astype(bf16)
        m0_ref[role] = jnp.concatenate([m0, m0], axis=0)
        mc_ref[role] = jnp.concatenate([mc, mc], axis=0)

    index_ref[...] = jnp.zeros((128, 128), f32)
    for f in range(6):
        index_ref[f : f + 1, 0:O] = fown_ref[f].astype(f32)
        index_ref[8 + f : 9 + f, 0:O] = foct_ref[f : f + 1].astype(f32)
        index_ref[16 + f : 17 + f, 0:O] = fco_ref[f : f + 1].astype(f32)
        index_ref[24 + f : 25 + f, 0:O] = fq_ref[f : f + 1].astype(f32)
    index_ref[32:33, :] = bown_ref[...].astype(f32)
    index_ref[33:34, :] = boct_ref[...].astype(f32)
    columns = index_ref[...].T.astype(i32)

    takes = face_slots(columns, me)
    oct_col = jnp.concatenate([columns[0:O, 8 + f : 9 + f] for f in range(6)], axis=0)
    lane_wide = iota((F6, 128), 1)
    row_face = iota((F6, 128), 0) // O
    wanted = jnp.where(
        lane_wide < S, (oct_col == lane_wide).astype(f32), (lane_wide - S == row_face).astype(f32)
    ).astype(bf16)

    block_delta = (columns[:, 32:33] - me + N) % N
    block_slot = slots_of((block_delta == offs_row).astype(f32))
    slot_lane = iota((B, ROWS), 1).astype(f32)
    into = [(block_slot + 4.0 * d == slot_lane).astype(f32).astype(bf16) for d in range(3)]
    oct_is = columns[:, 33:34] == iota((B, 128), 1)
    at_home = ((block_delta == 0) & oct_is).astype(f32).astype(bf16)
    oct_hot = oct_is.astype(f32).astype(bf16)
    req_send[:, 0:128] = dot_t(takes.astype(bf16), wanted).astype(bf16)
    req_send[:, 128:256] = dot_t(into[0] + into[1] + into[2], oct_hot).astype(bf16)

    for copy in loads:
        copy.wait()
    masses = mass_ref[...]
    tile = masses[0:8, 0:128]
    for r in range(16):
        for h in range(2):
            if r or h:
                tile = tile + masses[8 * r : 8 * r + 8, 128 * h : 128 * h + 128]

    def deposit(i, carry):
        rows = pl.ds(pl.multiple_of(i * 8, 8), 8)
        xs, ys, zs, ms = pos_ref[0, rows, :], pos_ref[1, rows, :], pos_ref[2, rows, :], mass_ref[rows, :]
        for r in range(8):
            wx = weights(xs[r : r + 1]) * ms[r : r + 1]
            high, low = crossed(weights(ys[r : r + 1]), weights(zs[r : r + 1]))
            x_high = wx.astype(bf16).astype(f32)
            left = jnp.concatenate([x_high, wx - x_high], axis=0).astype(bf16)
            right = jnp.concatenate([high, low], axis=0)
            both = lax.dot_general(
                left, right, (((1,), (1,)), ((), ())), preferred_element_type=f32
            )
            dep_ref[pl.ds(pl.multiple_of(i * 64 + 8 * r, 8), 8), :] = both[0:8] + both[8:16]
            cross_ref[pl.ds(pl.multiple_of(i * 1024 + 128 * r, 128), 128), :] = right
        return carry

    lax.fori_loop(0, B // 16, deposit, 0)

    pl.semaphore_wait(barrier, len(partners))

    requests = send_lanes(req_send, req_got, req_ss, req_rs, hosts)
    index_copy = send(index_ref.at[pl.ds(0, 32)], index_got, one_ss.at[0], one_rs.at[0], my_host)
    sums = []

    def sum_start(s, tile):
        sum_send[s] = tile
        for j, (p, back) in enumerate(stages[s]):
            at = first_sum[s]
            sums.append(
                send(sum_send.at[s], sum_got.at[at + back], sum_ss.at[at + j], sum_rs.at[at + back], p)
            )

    def sum_end(s, tile):
        at, count = first_sum[s], len(stages[s])
        for copy in sums[at : at + count]:
            copy.wait_recv()
        for j in range(count):
            tile = tile + sum_got[at + j]
        return tile

    sum_start(0, tile)

    lax.fori_loop(B // 16, B // 8, deposit, 0)

    low_half = iota((B, 128), 1) < S
    parts = []
    for i in range(4):
        even = dep_ref[pl.ds(2 * i, B, stride=8), :]
        odd = dep_ref[pl.ds(2 * i + 1, B, stride=8), :]
        parts.append(
            jnp.where(low_half, even + pltpu.roll(even, S, 1), odd + pltpu.roll(odd, S, 1))
        )
    rest = jnp.concatenate(parts, axis=1)
    pieces = []
    for _ in range(3):
        piece = rest.astype(bf16)
        rest = rest - piece.astype(f32)
        pieces.append(piece)
    stacked = jnp.concatenate(pieces, axis=0)
    msg_send[...] = dot_t(jnp.concatenate(into, axis=0), stacked).astype(bf16)
    deposits = send_lanes(msg_send, dep_got, msg_ss, dep_rs, hosts)
    home = dot_t(jnp.concatenate([at_home] * 3, axis=0), stacked)[0:O]
    home_send[...] = home.astype(bf16)
    home_copy = send(home_send, home_got, one_ss.at[1], one_rs.at[1], my_host)
    homelo_send[...] = (home - home.astype(bf16).astype(f32)).astype(bf16)
    homelo_copy = send(homelo_send, homelo_got, one_ss.at[4], one_rs.at[4], my_host)

    for d in range(3):
        pick_ref[:, 128 * d : 128 * d + 128] = pick_table(d)
        place_ref[256 * d : 256 * d + 256, :] = place_table(d)
    diag_ref[...] = (iota((F6, F6), 0) // S == iota((F6, F6), 1) // S).astype(f32).astype(bf16)
    to_face = (iota((128, F6), 0) - S == iota((128, F6), 1) // S).astype(f32).astype(bf16)

    tile = sum_end(0, tile)
    sum_start(1, tile)

    index_copy.wait_recv()
    spare = jnp.zeros((96, 128), f32)
    columns = jnp.concatenate([index_got[...], spare], axis=0).T.astype(i32)
    set_tables(0, columns, owner)

    for copy in requests:
        copy.wait_recv()
    asks = req_got[...]
    os_ref[...] = asks[:, 0:S]
    fmask_ref[...] = dot(asks[:, 0:128], to_face)
    slot_octs = asks[:, 128 : 128 + S]

    for copy in deposits:
        copy.wait_recv()
    density = dot_t(slot_octs, dep_got[...])
    home_copy.wait_recv()
    source = COUPLING * (density + home_got[...].astype(f32))
    dens_ref[...] = source
    work_ref[...] = source * (-1.0 / 6.0)

    lane = iota((1, C), 1)
    at = (lane // 64, lane // 8 % 8, lane % 8)
    strides = (64, 8, 1)

    def inner(phi, d):
        up = jnp.where(at[d] < 7, pltpu.roll(phi, C - strides[d], 1), 0.0)
        down = jnp.where(at[d] > 0, pltpu.roll(phi, strides[d], 1), 0.0)
        return up, down

    def placed(raw, d, sign=None, role=0):
        rows = raw.shape[0]
        part = raw[:, 128 * d : 128 * d + 128]
        if sign is not None:
            part = part * sign
        left = jnp.concatenate(
            [
                part * m0_ref[role, 0:rows, 128 * d : 128 * d + 128],
                part * mc_ref[role, 0:rows, 128 * d : 128 * d + 128],
            ],
            axis=1,
        )
        return dot(left, place_ref[256 * d : 256 * d + 256, :])

    def exchange_start(phi, slot):
        high = phi.astype(bf16)
        layers = dot(high, pick_ref[...]).astype(bf16)
        chosen = dot(os_ref[...], layers) * fmask_ref[...]
        out = chosen[:, 0:128] + chosen[:, 128:256] + chosen[:, 256:384]
        face_send[...] = (out + pltpu.roll(out, S, 1)).astype(bf16)
        copies = send_lanes(face_send, face_got.at[slot], face_ss, face_rs.at[slot], peers)
        return high, layers, copies

    def home_ghosts(phi, high, layers, role=0):
        low = (phi - high.astype(f32)).astype(bf16)
        layers_low = dot(low, pick_ref[...]).astype(bf16)
        diag = diag_ref[...]
        wide = [jnp.concatenate([x] * 6, axis=0) * diag for x in (layers, layers_low)]
        return jnp.concatenate([dot(home_ref[role], x).astype(bf16) for x in wide], axis=0)

    def away_ghosts(got, role=0):
        wide = jnp.concatenate([got] * 3, axis=1) * smask_ref[role]
        return dot(gro_ref[role], wide).astype(bf16)

    def sweep(slot, between):
        high, layers, copies = exchange_start(work_ref[...], slot)
        between()
        phi = work_ref[...]
        raw = home_ghosts(phi, high, layers)
        total = placed(raw, 0) + placed(raw, 1) + placed(raw, 2)
        total = total[0:O] + total[O : 2 * O] - dens_ref[...]
        for d in range(3):
            up, down = inner(phi, d)
            total = total + (up + down)
        for copy in copies:
            copy.wait_recv()
        raw = away_ghosts(face_got[slot])
        total = total + (placed(raw, 0) + placed(raw, 1) + placed(raw, 2))
        work_ref[...] = total * (1.0 / 6.0)
        for copy in copies:
            copy.wait_send()

    tiles = [tile]

    def step_sum(s):
        tiles.append(sum_end(s, tiles[-1]))
        if s < 3:
            sum_start(s + 1, tiles[-1])

    def add_low():
        homelo_copy.wait_recv()
        low = COUPLING * homelo_got[...].astype(f32)
        dens_ref[...] = dens_ref[...] + low
        work_ref[...] = work_ref[...] - low * (1.0 / 6.0)
        step_sum(1)

    sweep(1, add_low)
    def own_tables():
        step_sum(2)
        set_tables(1, index_ref[...].T.astype(i32), me)

    sweep(0, own_tables)
    sweep(1, lambda: step_sum(3))
    total = jnp.sum(jnp.sum(tiles[-1], axis=0, keepdims=True), axis=1, keepdims=True)
    mean = total * (COUPLING / TOTAL_CELLS)
    work_ref[...] = work_ref[...] + mean * (4.0 / 6.0)
    dens_ref[...] = dens_ref[...] - mean

    def later(k, carry):
        sweep(lax.rem(k, 2), lambda: None)
        return carry

    lax.fori_loop(4, 8, later, 0)

    for copy in deposits:
        copy.wait_send()
    phi = work_ref[...]
    high, layers, copies = exchange_start(phi, 0)
    phi_copy = send(work_ref, phi_got, one_ss.at[3], one_rs.at[3], owner)
    sign = jnp.where(iota((1, 128), 1) < S, 0.5, -0.5).astype(bf16)

    def near_field(phi, high, layers, role):
        raw = home_ghosts(phi, high, layers, role)
        parts = []
        for d in range(3):
            up, down = inner(phi, d)
            part = placed(raw, d, sign, role)
            parts.append(0.5 * (down - up) + part[0:O] + part[O : 2 * O])
        return parts

    def whole_field(local, got, role):
        raw = away_ghosts(got, role)
        return [(local[d] + placed(raw, d, sign, role)).astype(bf16) for d in range(3)]

    local = near_field(phi, high, layers, 0)
    for copy in copies:
        copy.wait_recv()
    layers_copy = send(face_got.at[0], layers_got, one_ss.at[2], one_rs.at[2], owner)
    field = whole_field(local, face_got[0], 0)
    row_dim = iota((ROWS, 1), 0) % 16 // 4
    picked = [dot(slot_octs, field[d]) for d in range(3)]
    msg_send[...] = jnp.where(
        row_dim == 0, picked[0], jnp.where(row_dim == 1, picked[1], picked[2])
    ).astype(bf16)
    returns = send_lanes(msg_send, field_got, msg_ss, field_rs, holders)

    phi_copy.wait_recv()
    own = phi_got[...]
    phi_ref[...] = own
    high = own.astype(bf16)
    local = near_field(own, high, dot(high, pick_ref[...]).astype(bf16), 1)
    layers_copy.wait_recv()
    field = whole_field(local, layers_got[...], 1)
    mine = [dot(at_home[:, 0:O], field[d]) for d in range(3)]
    for copy in returns:
        copy.wait_recv()
    got = field_got[...]
    for d in range(3):
        values = mine[d] + dot(into[d], got)
        for i in range(4):
            pair = values[:, 128 * i : 128 * i + 128]
            turned = pltpu.roll(pair, S, 1)
            field_ref[d, pl.ds(2 * i, B, stride=8), :] = jnp.where(low_half, pair, turned)
            field_ref[d, pl.ds(2 * i + 1, B, stride=8), :] = jnp.where(low_half, turned, pair)

    def interpolate(i, carry):
        rows = pl.ds(pl.multiple_of(i * 8, 8), 8)
        xs = pos_ref[0, rows, :]
        out = [[], [], []]
        for r in range(8):
            wx = weights(xs[r : r + 1])
            both = cross_ref[pl.ds(pl.multiple_of(i * 1024 + 128 * r, 128), 128), :]
            at = pl.ds(pl.multiple_of(i * 64 + 8 * r, 8), 8)
            left = jnp.concatenate([field_ref[d, at, :] for d in range(3)], axis=0).astype(bf16)
            value = dot(left, both)
            for d in range(3):
                out[d].append(jnp.sum(value[8 * d : 8 * d + 8] * wx, axis=0, keepdims=True))
        for d in range(3):
            accel_ref[d, rows, :] = jnp.concatenate(out[d], axis=0)
        return carry

    lax.fori_loop(0, B // 8, interpolate, 0)

    for copy in [index_copy, home_copy, homelo_copy, phi_copy, layers_copy] + requests + sums + copies + returns:
        copy.wait_send()


def on_device(
    positions, masses, block_owner, block_oct, face_owner, face_oct, face_coarse, face_quadrant
):
    dma = pltpu.SemaphoreType.DMA
    vmem = pl.BlockSpec(memory_space=pltpu.VMEM)
    potential, accel = pl.pallas_call(
        kernel,
        out_shape=(
            jax.ShapeDtypeStruct((O, C), f32),
            jax.ShapeDtypeStruct((3, B, PART), f32),
        ),
        in_specs=[pl.BlockSpec(memory_space=pl.ANY)] * 2 + [vmem] * 6,
        out_specs=(vmem, vmem),
        scratch_shapes=[
            pltpu.VMEM((B * 8, 128), f32),
            pltpu.VMEM((ROWS, 256), bf16),
            pltpu.VMEM((ROWS, 256), bf16),
            pltpu.VMEM((ROWS, C), bf16),
            pltpu.VMEM((ROWS, C), bf16),
            pltpu.VMEM((ROWS, C), bf16),
            pltpu.VMEM((ROWS, 128), bf16),
            pltpu.VMEM((2, ROWS, 128), bf16),
            pltpu.VMEM((4, 8, 128), f32),
            pltpu.VMEM((10, 8, 128), f32),
            pltpu.VMEM((3, B * 8, 128), f32),
            pltpu.VMEM((O, C), f32),
            pltpu.VMEM((2, 2 * O, F6), bf16),
            pltpu.VMEM((2, 2 * O, F6), bf16),
            pltpu.VMEM((2, O, F6), bf16),
            pltpu.VMEM((ROWS, F6), f32),
            pltpu.VMEM((2, ROWS, F6), bf16),
            pltpu.VMEM((2, O, ROWS), bf16),
            pltpu.VMEM((ROWS, S), bf16),
            pltpu.VMEM((C, F6), bf16),
            pltpu.VMEM((768, C), bf16),
            pltpu.VMEM((F6, F6), bf16),
            pltpu.VMEM((128, 128), f32),
            pltpu.VMEM((32, 128), f32),
            pltpu.VMEM((O, C), bf16),
            pltpu.VMEM((O, C), bf16),
            pltpu.VMEM((ROWS, 128), bf16),
            pltpu.VMEM((O, C), f32),
            pltpu.VMEM((O, C), f32),
            pltpu.VMEM((3, B, PART), f32),
            pltpu.VMEM((B, PART), f32),
            pltpu.VMEM((B * 128, PART), bf16),
            pltpu.VMEM((O, C), bf16),
            pltpu.VMEM((O, C), bf16),
            dma((LANES,)),
            dma((LANES,)),
            dma((LANES,)),
            dma((LANES,)),
            dma((LANES,)),
            dma((LANES,)),
            dma((2, LANES)),
            dma((10,)),
            dma((10,)),
            dma((5,)),
            dma((5,)),
            dma((2,)),
        ],
        compiler_params=pltpu.CompilerParams(
            collective_id=0, has_side_effects=True, vmem_limit_bytes=56 * 1024 * 1024
        ),
    )(
        jnp.transpose(positions, (1, 0, 2)),
        masses,
        block_owner.T,
        block_oct[None, :],
        jnp.transpose(face_owner, (1, 2, 0)),
        face_oct.T,
        face_coarse.T,
        face_quadrant.T,
    )
    return potential, jnp.transpose(accel, (1, 0, 2))


def solution(mesh):
    placed = (
        P("hilbert", None, None),
        P("hilbert", None),
        P("hilbert", None),
        P("hilbert"),
        P("hilbert", None, None),
        P("hilbert", None),
        P("hilbert", None),
        P("hilbert", None),
    )
    return jax.shard_map(
        on_device,
        mesh=mesh,
        in_specs=placed,
        out_specs=(P("hilbert", None), P("hilbert", None, None)),
        check_vma=False,
    )
```

```python
import jax
import jax.numpy as jnp
from jax import lax
from jax.experimental import pallas as pl
from jax.experimental.pallas import tpu as pltpu
from jax.sharding import PartitionSpec as P

N = 128
B = 128
O = 64
C = 512
S = 64
F6 = 6 * S
PART = 256
OFFS = (1, 2, 3, 4, 127, 126, 125, 124, 64)
BACK = (4, 5, 6, 7, 0, 1, 2, 3, 8)
LANES = len(OFFS)
LANE_ORDER = (8, 3, 7, 2, 6, 1, 5, 0, 4)
ROWS = 16 * LANES
TOTAL_CELLS = float(N * O * C)
COUPLING = 0.25

f32 = jnp.float32
bf16 = jnp.bfloat16
i32 = jnp.int32


def dot(a, b):
    return jnp.dot(a, b, preferred_element_type=f32)


def dot_t(a, b):
    return lax.dot_general(a, b, (((0,), (0,)), ((), ())), preferred_element_type=f32)


def iota(shape, dim):
    return lax.broadcasted_iota(i32, shape, dim)


def pick_table(d):
    cell, lane = iota((C, 128), 0), iota((C, 128), 1)
    coord, spot = cell_spot(cell, d)
    return ((coord == jnp.where(lane < S, 7, 0)) & (spot == lane % S)).astype(f32).astype(bf16)


def place_table(d):
    row, cell = iota((256, C), 0), iota((256, C), 1)
    coord, spot = cell_spot(cell, d)
    j = row % S
    here = coord == (row // S % 2) * 7
    fine = spot == j
    coarse = ((spot // 16) == (j // 8 % 4)) & ((spot % 8) // 2 == j % 4)
    return (here & (((row < 128) & fine) | ((row >= 128) & coarse))).astype(f32).astype(bf16)


def cell_spot(cell, d):
    x, y, z = cell // 64, cell // 8 % 8, cell % 8
    return ((x, y * 8 + z), (y, x * 8 + z), (z, x * 8 + y))[d]


def weights(row):
    centres = iota((8, PART), 0).astype(f32) + 0.5
    return jnp.maximum(0.0, 1.0 - jnp.abs(row - centres))


def crossed(wy, wz):
    full = jnp.concatenate([wy[y : y + 1] * wz for y in range(8)], axis=0)
    high = full.astype(bf16)
    return high, (full - high.astype(f32)).astype(bf16)


def device_at(x, z, y, core):
    return x * 32 + z * 8 + y * 2 + core


def host_of(i):
    x, z, y = i // 32, lax.rem(i // 8, 4), lax.rem(i // 2, 4)
    return device_at(
        lax.rem(x + 3, 4),
        z + lax.rem(x, 2) * (3 - 2 * z),
        y + lax.rem(z, 2) * (3 - 2 * y),
        lax.rem(i, 2),
    )


def hosted_by(i):
    x, z, y = lax.rem(i // 32 + 1, 4), lax.rem(i // 8, 4), lax.rem(i // 2, 4)
    z = z + lax.rem(x, 2) * (3 - 2 * z)
    return device_at(x, z, y + lax.rem(z, 2) * (3 - 2 * y), lax.rem(i, 2))


def kernel(
    pos_hbm, mass_hbm, bown_ref, boct_ref, fown_ref, foct_ref, fco_ref, fq_ref,
    phi_ref, accel_ref,
    dep_ref, req_send, req_got, msg_send, dep_got, field_got, face_send, face_got,
    sum_send, sum_got, field_ref, dens_ref, m0_ref, mc_ref, home_ref, fmask_ref, smask_ref, gro_ref, os_ref,
    pick_ref, place_ref, diag_ref, index_ref, index_got, home_send, home_got, layers_got,
    work_ref, phi_got, pos_ref, mass_ref, cross_ref, homelo_send, homelo_got,
    slots_ref, m0s_ref, mcs_ref, next_ref,
    req_ss, req_rs, msg_ss, dep_rs, field_rs, face_ss, face_rs, sum_ss, sum_rs, one_ss, one_rs, load_sem,
):
    me = lax.axis_index("hilbert")
    owner = hosted_by(me)
    my_host = host_of(me)
    near = [lax.rem(me + o, N) for o in OFFS]
    hosts = [host_of(p) for p in near]
    holders = [lax.rem(owner + o, N) for o in OFFS]
    peers = [host_of(p) for p in holders]
    stages = []
    for stride, size in ((1, 2), (2, 4), (8, 4), (32, 4)):
        digit = lax.rem(me // stride, size)
        stages.append(
            [(me + (lax.rem(digit + j, size) - digit) * stride, size - 1 - j) for j in range(1, size)]
        )
    first_sum = (0, 1, 4, 7)

    barrier = pltpu.get_barrier_semaphore()
    partners = peers + hosts + holders + [my_host, owner] + [p for stage in stages for p, _ in stage]
    for p in partners:
        pl.semaphore_signal(barrier, inc=1, device_id=(p,), device_id_type=pl.DeviceIdType.MESH)

    loads = [
        pltpu.make_async_copy(mass_hbm, mass_ref, load_sem.at[0]),
        pltpu.make_async_copy(pos_hbm, pos_ref, load_sem.at[1]),
    ]
    for copy in loads:
        copy.start()

    def send(src, dst, ss, rs, p):
        copy = pltpu.make_async_remote_copy(
            src_ref=src, dst_ref=dst, send_sem=ss, recv_sem=rs,
            device_id=(p,), device_id_type=pl.DeviceIdType.MESH,
        )
        copy.start()
        return copy

    def send_lanes(src, dst, ss, rs, to):
        return [
            send(
                src.at[pl.ds(16 * l, 16)], dst.at[pl.ds(16 * BACK[l], 16)],
                ss.at[l], rs.at[BACK[l]], to[l],
            )
            for l in LANE_ORDER
        ]

    lane128 = iota((1, 128), 1)
    offs_row = jnp.where(
        lane128 < 4,
        lane128 + 1,
        jnp.where(lane128 < 8, 131 - lane128, jnp.where(lane128 == 8, 64, -1)),
    )
    lane_f = lane128.astype(f32)

    def slots_of(match):
        rows = match.shape[0]
        earlier = (iota((rows, rows), 0) > iota((rows, rows), 1)).astype(f32).astype(bf16)
        rank = jnp.sum(dot(earlier, match.astype(bf16)) * match, axis=1, keepdims=True)
        lane = jnp.sum(match * lane_f, axis=1, keepdims=True)
        away = jnp.sum(match, axis=1, keepdims=True)
        return jnp.where(away > 0.5, lane * 16.0 + rank, -1000.0)

    def face_slots(columns, of):
        delta = (columns[0:O, 0:6] - of + N) % N
        match = jnp.concatenate(
            [(delta[:, f : f + 1] == offs_row).astype(f32) for f in range(6)], axis=0
        )
        return (slots_of(match) == iota((F6, ROWS), 1).astype(f32)).astype(f32)

    def set_tables(role, columns, of):
        group = iota((O, F6), 1) // S
        inside = iota((O, F6), 1) % S

        def spread(base):
            total = jnp.zeros((O, F6), i32)
            for f in range(6):
                total = jnp.where(group == f, columns[0:O, base + f : base + f + 1], total)
            return total

        takes = face_slots(columns, of)
        gro = takes[0:O]
        for f in range(1, 6):
            gro = gro + takes[f * O : (f + 1) * O]
        gro_ref[role] = gro.astype(bf16)
        same_face = (iota((F6, F6), 0) // O == iota((F6, F6), 1) // S).astype(f32).astype(bf16)
        smask_ref[role] = dot_t(takes.astype(bf16), same_face).astype(bf16)
        home_ref[role] = ((spread(0) == of) & (spread(8) == inside)).astype(f32).astype(bf16)
        coarse_x = spread(16)
        quad_x = spread(24)
        quad_in = (inside // 32) * 2 + (inside % 8) // 4
        m0 = (coarse_x != 1).astype(f32).astype(bf16)
        mc = ((coarse_x == 1) & (quad_x == quad_in)).astype(f32).astype(bf16)
        m0_ref[role] = jnp.concatenate([m0, m0], axis=0)
        mc_ref[role] = jnp.concatenate([mc, mc], axis=0)

    index_ref[...] = jnp.zeros((128, 128), f32)
    for f in range(6):
        index_ref[f : f + 1, 0:O] = fown_ref[f].astype(f32)
        index_ref[8 + f : 9 + f, 0:O] = foct_ref[f : f + 1].astype(f32)
        index_ref[16 + f : 17 + f, 0:O] = fco_ref[f : f + 1].astype(f32)
        index_ref[24 + f : 25 + f, 0:O] = fq_ref[f : f + 1].astype(f32)
    index_ref[32:33, :] = bown_ref[...].astype(f32)
    index_ref[33:34, :] = boct_ref[...].astype(f32)
    columns = index_ref[...].T.astype(i32)

    takes = face_slots(columns, me)
    oct_col = jnp.concatenate([columns[0:O, 8 + f : 9 + f] for f in range(6)], axis=0)
    lane_wide = iota((F6, 128), 1)
    row_face = iota((F6, 128), 0) // O
    wanted = jnp.where(
        lane_wide < S, (oct_col == lane_wide).astype(f32), (lane_wide - S == row_face).astype(f32)
    ).astype(bf16)

    block_delta = (columns[:, 32:33] - me + N) % N
    block_slot = slots_of((block_delta == offs_row).astype(f32))
    slot_lane = iota((B, ROWS), 1).astype(f32)
    into = [(block_slot + 4.0 * d == slot_lane).astype(f32).astype(bf16) for d in range(3)]
    oct_is = columns[:, 33:34] == iota((B, 128), 1)
    at_home = ((block_delta == 0) & oct_is).astype(f32).astype(bf16)
    oct_hot = oct_is.astype(f32).astype(bf16)
    req_send[:, 0:128] = dot_t(takes.astype(bf16), wanted).astype(bf16)
    req_send[:, 128:256] = dot_t(into[0] + into[1] + into[2], oct_hot).astype(bf16)

    for copy in loads:
        copy.wait()
    masses = mass_ref[...]
    tile = masses[0:8, 0:128]
    for r in range(16):
        for h in range(2):
            if r or h:
                tile = tile + masses[8 * r : 8 * r + 8, 128 * h : 128 * h + 128]

    def deposit(i, carry):
        rows = pl.ds(pl.multiple_of(i * 8, 8), 8)
        xs, ys, zs, ms = pos_ref[0, rows, :], pos_ref[1, rows, :], pos_ref[2, rows, :], mass_ref[rows, :]
        for r in range(8):
            wx = weights(xs[r : r + 1]) * ms[r : r + 1]
            high, low = crossed(weights(ys[r : r + 1]), weights(zs[r : r + 1]))
            x_high = wx.astype(bf16).astype(f32)
            left = jnp.concatenate([x_high, wx - x_high], axis=0).astype(bf16)
            right = jnp.concatenate([high, low], axis=0)
            both = lax.dot_general(
                left, right, (((1,), (1,)), ((), ())), preferred_element_type=f32
            )
            dep_ref[pl.ds(pl.multiple_of(i * 64 + 8 * r, 8), 8), :] = both[0:8] + both[8:16]
            cross_ref[pl.ds(pl.multiple_of(i * 1024 + 128 * r, 128), 128), :] = right
        return carry

    lax.fori_loop(0, B // 16, deposit, 0)

    pl.semaphore_wait(barrier, len(partners))

    requests = send_lanes(req_send, req_got, req_ss, req_rs, hosts)
    index_copy = send(index_ref.at[pl.ds(0, 32)], index_got, one_ss.at[0], one_rs.at[0], my_host)
    sums = []

    def sum_start(s, tile):
        sum_send[s] = tile
        for j, (p, back) in enumerate(stages[s]):
            at = first_sum[s]
            sums.append(
                send(sum_send.at[s], sum_got.at[at + back], sum_ss.at[at + j], sum_rs.at[at + back], p)
            )

    def sum_end(s, tile):
        at, count = first_sum[s], len(stages[s])
        for copy in sums[at : at + count]:
            copy.wait_recv()
        for j in range(count):
            tile = tile + sum_got[at + j]
        return tile

    sum_start(0, tile)

    lax.fori_loop(B // 16, B // 8, deposit, 0)

    low_half = iota((B, 128), 1) < S
    parts = []
    for i in range(4):
        even = dep_ref[pl.ds(2 * i, B, stride=8), :]
        odd = dep_ref[pl.ds(2 * i + 1, B, stride=8), :]
        parts.append(
            jnp.where(low_half, even + pltpu.roll(even, S, 1), odd + pltpu.roll(odd, S, 1))
        )
    rest = jnp.concatenate(parts, axis=1)
    pieces = []
    for _ in range(3):
        piece = rest.astype(bf16)
        rest = rest - piece.astype(f32)
        pieces.append(piece)
    stacked = jnp.concatenate(pieces, axis=0)
    msg_send[...] = dot_t(jnp.concatenate(into, axis=0), stacked).astype(bf16)
    deposits = send_lanes(msg_send, dep_got, msg_ss, dep_rs, hosts)
    home = dot_t(jnp.concatenate([at_home] * 3, axis=0), stacked)[0:O]
    home_send[...] = home.astype(bf16)
    home_copy = send(home_send, home_got, one_ss.at[1], one_rs.at[1], my_host)
    homelo_send[...] = (home - home.astype(bf16).astype(f32)).astype(bf16)
    homelo_copy = send(homelo_send, homelo_got, one_ss.at[4], one_rs.at[4], my_host)

    for d in range(3):
        pick_ref[:, 128 * d : 128 * d + 128] = pick_table(d)
        place_ref[256 * d : 256 * d + 256, :] = place_table(d)
    for d in range(3):
        rows = slice(256 * d, 256 * d + 256)
        next_ref[rows, :] = dot(place_ref[rows, :], pick_ref[...]).astype(bf16)
    diag_ref[...] = (iota((F6, F6), 0) // S == iota((F6, F6), 1) // S).astype(f32).astype(bf16)
    to_face = (iota((128, F6), 0) - S == iota((128, F6), 1) // S).astype(f32).astype(bf16)

    tile = sum_end(0, tile)
    sum_start(1, tile)

    index_copy.wait_recv()
    spare = jnp.zeros((96, 128), f32)
    columns = jnp.concatenate([index_got[...], spare], axis=0).T.astype(i32)
    set_tables(0, columns, owner)

    for copy in requests:
        copy.wait_recv()
    asks = req_got[...]
    os_ref[...] = asks[:, 0:S]
    fmask_ref[...] = dot(asks[:, 0:128], to_face)
    slot_octs = asks[:, 128 : 128 + S]

    for copy in deposits:
        copy.wait_recv()
    density = dot_t(slot_octs, dep_got[...])
    home_copy.wait_recv()
    source = COUPLING * (density + home_got[...].astype(f32))
    dens_ref[...] = source
    work_ref[...] = source * (-1.0 / 6.0)

    lane = iota((1, C), 1)
    at = (lane // 64, lane // 8 % 8, lane % 8)
    strides = (64, 8, 1)

    def inner(phi, d):
        up = jnp.where(at[d] < 7, pltpu.roll(phi, C - strides[d], 1), 0.0)
        down = jnp.where(at[d] > 0, pltpu.roll(phi, strides[d], 1), 0.0)
        return up, down

    def placed(raw, d, sign=None, role=0):
        rows = raw.shape[0]
        part = raw[:, 128 * d : 128 * d + 128]
        if sign is not None:
            part = part * sign
        left = jnp.concatenate(
            [
                part * m0_ref[role, 0:rows, 128 * d : 128 * d + 128],
                part * mc_ref[role, 0:rows, 128 * d : 128 * d + 128],
            ],
            axis=1,
        )
        return dot(left, place_ref[256 * d : 256 * d + 256, :])

    def face_copies(slot):
        return [
            pltpu.make_async_remote_copy(
                src_ref=face_send.at[pl.ds(16 * l, 16)],
                dst_ref=face_got.at[slot, pl.ds(16 * BACK[l], 16)],
                send_sem=face_ss.at[l], recv_sem=face_rs.at[slot, BACK[l]],
                device_id=(peers[l],), device_id_type=pl.DeviceIdType.MESH,
            )
            for l in LANE_ORDER
        ]

    def send_faces(chosen, slot):
        chosen = chosen * fmask_ref[...]
        out = chosen[:, 0:128] + chosen[:, 128:256] + chosen[:, 256:384]
        face_send[...] = (out + pltpu.roll(out, S, 1)).astype(bf16)
        for copy in face_copies(slot):
            copy.start()

    def layers_of(values):
        high = values.astype(bf16)
        low = (values - high.astype(f32)).astype(bf16)
        return [dot(x, pick_ref[...]).astype(bf16) for x in (high, low)]

    def home_ghosts(layers, role=0):
        diag = diag_ref[...]
        wide = [jnp.concatenate([x] * 6, axis=0) * diag for x in layers]
        return jnp.concatenate([dot(home_ref[role], x).astype(bf16) for x in wide], axis=0)

    def both_masks(part, d, fine, coarse):
        cols = slice(128 * d, 128 * d + 128)
        return jnp.concatenate([part * fine[:, cols], part * coarse[:, cols]], axis=1)

    def away_ghosts(got, role=0):
        wide = jnp.concatenate([got] * 3, axis=1) * smask_ref[role]
        return dot(gro_ref[role], wide).astype(bf16)

    def sweep(slot, later_slot, between, shift=None):
        between()
        phi = work_ref[...]
        raw = home_ghosts(layers_of(phi))
        total = placed(raw, 0) + placed(raw, 1) + placed(raw, 2)
        total = total[0:O] + total[O : 2 * O] - dens_ref[...]
        for d in range(3):
            up, down = inner(phi, d)
            total = total + (up + down)
        parts = layers_of(total)
        chosen = dot(os_ref[...], parts[0]) + dot(os_ref[...], parts[1])
        copies = face_copies(slot)
        for copy in copies:
            copy.wait_recv()
        got = face_got[slot]
        wide = jnp.concatenate([got] * 3, axis=1) * smask_ref[0]
        raw = dot(slots_ref[...], wide).astype(bf16)
        for d in range(3):
            left = both_masks(raw[:, 128 * d : 128 * d + 128], d, m0s_ref, mcs_ref)
            chosen = chosen + dot(left, next_ref[256 * d : 256 * d + 256, :])
        chosen = chosen * (1.0 / 6.0)
        if shift is not None:
            chosen = chosen + shift()
        for copy in copies:
            copy.wait_send()
        send_faces(chosen, later_slot)
        raw = away_ghosts(got)
        total = total + (placed(raw, 0) + placed(raw, 1) + placed(raw, 2))
        work_ref[...] = total * (1.0 / 6.0)

    tiles = [tile]

    def step_sum(s):
        tiles.append(sum_end(s, tiles[-1]))
        if s < 3:
            sum_start(s + 1, tiles[-1])

    def mean_of_all():
        total = jnp.sum(jnp.sum(tiles[-1], axis=0, keepdims=True), axis=1, keepdims=True)
        return total * (COUPLING / TOTAL_CELLS)

    def add_low():
        homelo_copy.wait_recv()
        low = COUPLING * homelo_got[...].astype(f32)
        dens_ref[...] = dens_ref[...] + low
        work_ref[...] = work_ref[...] - low * (1.0 / 6.0)
        step_sum(1)
        slots_ref[...] = dot(os_ref[...], gro_ref[0]).astype(bf16)
        m0s_ref[...] = dot(os_ref[...], m0_ref[0, 0:O, :]).astype(bf16)
        mcs_ref[...] = dot(os_ref[...], mc_ref[0, 0:O, :]).astype(bf16)

    first = work_ref[...].astype(bf16)
    send_faces(dot(os_ref[...], dot(first, pick_ref[...]).astype(bf16)), 1)
    sweep(1, 2, add_low)
    def own_tables():
        step_sum(2)
        set_tables(1, index_ref[...].T.astype(i32), me)

    sweep(2, 0, own_tables)
    sweep(0, 1, lambda: step_sum(3), lambda: mean_of_all() * (4.0 / 6.0))
    mean = mean_of_all()
    work_ref[...] = work_ref[...] + mean * (4.0 / 6.0)
    dens_ref[...] = dens_ref[...] - mean

    def later(k, carry):
        sweep(lax.rem(k, 3), lax.rem(k + 1, 3), lambda: None)
        return carry

    lax.fori_loop(4, 8, later, 0)

    for copy in deposits:
        copy.wait_send()
    phi = work_ref[...]
    phi_copy = send(work_ref, phi_got, one_ss.at[3], one_rs.at[3], owner)
    sign = jnp.where(iota((1, 128), 1) < S, 0.5, -0.5).astype(bf16)

    def near_field(phi, role):
        raw = home_ghosts(layers_of(phi), role)
        parts = []
        for d in range(3):
            up, down = inner(phi, d)
            part = placed(raw, d, sign, role)
            parts.append(0.5 * (down - up) + part[0:O] + part[O : 2 * O])
        return parts

    def whole_field(local, got, role):
        raw = away_ghosts(got, role)
        return [(local[d] + placed(raw, d, sign, role)).astype(bf16) for d in range(3)]

    local = near_field(phi, 0)
    copies = face_copies(2)
    for copy in copies:
        copy.wait_recv()
    layers_copy = send(face_got.at[2], layers_got, one_ss.at[2], one_rs.at[2], owner)
    field = whole_field(local, face_got[2], 0)
    row_dim = iota((ROWS, 1), 0) % 16 // 4
    picked = [dot(slot_octs, field[d]) for d in range(3)]
    msg_send[...] = jnp.where(
        row_dim == 0, picked[0], jnp.where(row_dim == 1, picked[1], picked[2])
    ).astype(bf16)
    returns = send_lanes(msg_send, field_got, msg_ss, field_rs, holders)

    phi_copy.wait_recv()
    own = phi_got[...]
    phi_ref[...] = own
    local = near_field(own, 1)
    layers_copy.wait_recv()
    field = whole_field(local, layers_got[...], 1)
    mine = [dot(at_home[:, 0:O], field[d]) for d in range(3)]
    for copy in returns:
        copy.wait_recv()
    got = field_got[...]
    for d in range(3):
        values = mine[d] + dot(into[d], got)
        for i in range(4):
            pair = values[:, 128 * i : 128 * i + 128]
            turned = pltpu.roll(pair, S, 1)
            field_ref[d, pl.ds(2 * i, B, stride=8), :] = jnp.where(low_half, pair, turned)
            field_ref[d, pl.ds(2 * i + 1, B, stride=8), :] = jnp.where(low_half, turned, pair)

    def interpolate(i, carry):
        rows = pl.ds(pl.multiple_of(i * 8, 8), 8)
        xs = pos_ref[0, rows, :]
        out = [[], [], []]
        for r in range(8):
            wx = weights(xs[r : r + 1])
            both = cross_ref[pl.ds(pl.multiple_of(i * 1024 + 128 * r, 128), 128), :]
            at = pl.ds(pl.multiple_of(i * 64 + 8 * r, 8), 8)
            left = jnp.concatenate([field_ref[d, at, :] for d in range(3)], axis=0).astype(bf16)
            value = dot(left, both)
            for d in range(3):
                out[d].append(jnp.sum(value[8 * d : 8 * d + 8] * wx, axis=0, keepdims=True))
        for d in range(3):
            accel_ref[d, rows, :] = jnp.concatenate(out[d], axis=0)
        return carry

    lax.fori_loop(0, B // 8, interpolate, 0)

    for copy in [index_copy, home_copy, homelo_copy, phi_copy, layers_copy] + requests + sums + copies + returns:
        copy.wait_send()


def on_device(
    positions, masses, block_owner, block_oct, face_owner, face_oct, face_coarse, face_quadrant
):
    dma = pltpu.SemaphoreType.DMA
    vmem = pl.BlockSpec(memory_space=pltpu.VMEM)
    potential, accel = pl.pallas_call(
        kernel,
        out_shape=(
            jax.ShapeDtypeStruct((O, C), f32),
            jax.ShapeDtypeStruct((3, B, PART), f32),
        ),
        in_specs=[pl.BlockSpec(memory_space=pl.ANY)] * 2 + [vmem] * 6,
        out_specs=(vmem, vmem),
        scratch_shapes=[
            pltpu.VMEM((B * 8, 128), f32),
            pltpu.VMEM((ROWS, 256), bf16),
            pltpu.VMEM((ROWS, 256), bf16),
            pltpu.VMEM((ROWS, C), bf16),
            pltpu.VMEM((ROWS, C), bf16),
            pltpu.VMEM((ROWS, C), bf16),
            pltpu.VMEM((ROWS, 128), bf16),
            pltpu.VMEM((3, ROWS, 128), bf16),
            pltpu.VMEM((4, 8, 128), f32),
            pltpu.VMEM((10, 8, 128), f32),
            pltpu.VMEM((3, B * 8, 128), f32),
            pltpu.VMEM((O, C), f32),
            pltpu.VMEM((2, 2 * O, F6), bf16),
            pltpu.VMEM((2, 2 * O, F6), bf16),
            pltpu.VMEM((2, O, F6), bf16),
            pltpu.VMEM((ROWS, F6), f32),
            pltpu.VMEM((2, ROWS, F6), bf16),
            pltpu.VMEM((2, O, ROWS), bf16),
            pltpu.VMEM((ROWS, S), bf16),
            pltpu.VMEM((C, F6), bf16),
            pltpu.VMEM((768, C), bf16),
            pltpu.VMEM((F6, F6), bf16),
            pltpu.VMEM((128, 128), f32),
            pltpu.VMEM((32, 128), f32),
            pltpu.VMEM((O, C), bf16),
            pltpu.VMEM((O, C), bf16),
            pltpu.VMEM((ROWS, 128), bf16),
            pltpu.VMEM((O, C), f32),
            pltpu.VMEM((O, C), f32),
            pltpu.VMEM((3, B, PART), f32),
            pltpu.VMEM((B, PART), f32),
            pltpu.VMEM((B * 128, PART), bf16),
            pltpu.VMEM((O, C), bf16),
            pltpu.VMEM((O, C), bf16),
            pltpu.VMEM((ROWS, ROWS), bf16),
            pltpu.VMEM((ROWS, F6), bf16),
            pltpu.VMEM((ROWS, F6), bf16),
            pltpu.VMEM((768, F6), bf16),
            dma((LANES,)),
            dma((LANES,)),
            dma((LANES,)),
            dma((LANES,)),
            dma((LANES,)),
            dma((LANES,)),
            dma((3, LANES)),
            dma((10,)),
            dma((10,)),
            dma((5,)),
            dma((5,)),
            dma((2,)),
        ],
        compiler_params=pltpu.CompilerParams(
            collective_id=0, has_side_effects=True, vmem_limit_bytes=54528 * 1024
        ),
    )(
        jnp.transpose(positions, (1, 0, 2)),
        masses,
        block_owner.T,
        block_oct[None, :],
        jnp.transpose(face_owner, (1, 2, 0)),
        face_oct.T,
        face_coarse.T,
        face_quadrant.T,
    )
    return potential, jnp.transpose(accel, (1, 0, 2))


def solution(mesh):
    placed = (
        P("hilbert", None, None),
        P("hilbert", None),
        P("hilbert", None),
        P("hilbert"),
        P("hilbert", None, None),
        P("hilbert", None),
        P("hilbert", None),
        P("hilbert", None),
    )
    return jax.shard_map(
        on_device,
        mesh=mesh,
        in_specs=placed,
        out_specs=(P("hilbert", None), P("hilbert", None, None)),
        check_vma=False,
    )
```

```python
import jax
import jax.numpy as jnp
from jax import lax
from jax.experimental import pallas as pl
from jax.experimental.pallas import tpu as pltpu
from jax.sharding import PartitionSpec as P

N = 128
B = 128
O = 64
C = 512
S = 64
F6 = 6 * S
PART = 256
OFFS = (1, 2, 3, 4, 127, 126, 125, 124, 64)
BACK = (4, 5, 6, 7, 0, 1, 2, 3, 8)
LANES = len(OFFS)
LANE_ORDER = (8, 3, 7, 2, 6, 1, 5, 0, 4)
ROWS = 16 * LANES
TOTAL_CELLS = float(N * O * C)
COUPLING = 0.25

f32 = jnp.float32
bf16 = jnp.bfloat16
i32 = jnp.int32


def dot(a, b):
    return jnp.dot(a, b, preferred_element_type=f32)


def dot_t(a, b):
    return lax.dot_general(a, b, (((0,), (0,)), ((), ())), preferred_element_type=f32)


def iota(shape, dim):
    return lax.broadcasted_iota(i32, shape, dim)


def pick_table(d):
    cell, lane = iota((C, 128), 0), iota((C, 128), 1)
    coord, spot = cell_spot(cell, d)
    return ((coord == jnp.where(lane < S, 7, 0)) & (spot == lane % S)).astype(f32).astype(bf16)


def place_table(d):
    row, cell = iota((256, C), 0), iota((256, C), 1)
    coord, spot = cell_spot(cell, d)
    j = row % S
    here = coord == (row // S % 2) * 7
    fine = spot == j
    coarse = ((spot // 16) == (j // 8 % 4)) & ((spot % 8) // 2 == j % 4)
    return (here & (((row < 128) & fine) | ((row >= 128) & coarse))).astype(f32).astype(bf16)


def cell_spot(cell, d):
    x, y, z = cell // 64, cell // 8 % 8, cell % 8
    return ((x, y * 8 + z), (y, x * 8 + z), (z, x * 8 + y))[d]


def weights(row):
    centres = iota((8, PART), 0).astype(f32) + 0.5
    return jnp.maximum(0.0, 1.0 - jnp.abs(row - centres))


def crossed(wy, wz):
    full = jnp.concatenate([wy[y : y + 1] * wz for y in range(8)], axis=0)
    high = full.astype(bf16)
    return high, (full - high.astype(f32)).astype(bf16)


def device_at(x, z, y, core):
    return x * 32 + z * 8 + y * 2 + core


def host_of(i):
    x, z, y = i // 32, lax.rem(i // 8, 4), lax.rem(i // 2, 4)
    return device_at(
        lax.rem(x + 3, 4),
        z + lax.rem(x, 2) * (3 - 2 * z),
        y + lax.rem(z, 2) * (3 - 2 * y),
        lax.rem(i, 2),
    )


def hosted_by(i):
    x, z, y = lax.rem(i // 32 + 1, 4), lax.rem(i // 8, 4), lax.rem(i // 2, 4)
    z = z + lax.rem(x, 2) * (3 - 2 * z)
    return device_at(x, z, y + lax.rem(z, 2) * (3 - 2 * y), lax.rem(i, 2))


def kernel(
    pos_hbm, mass_hbm, bown_ref, boct_ref, fown_ref, foct_ref, fco_ref, fq_ref,
    phi_ref, accel_ref,
    dep_ref, req_send, req_got, msg_send, dep_got, field_got, face_send, face_got,
    sum_send, sum_got, field_ref, dens_ref, m0_ref, mc_ref, home_ref, fmask_ref, smask_ref, gro_ref, os_ref,
    pick_ref, place_ref, diag_ref, index_ref, index_got, home_send, home_got, layers_got,
    work_ref, phi_got, pos_ref, mass_ref, cross_ref, homelo_send, homelo_got,
    slots_ref, m0s_ref, mcs_ref, next_ref,
    req_ss, req_rs, msg_ss, dep_rs, field_rs, face_ss, face_rs, sum_ss, sum_rs, one_ss, one_rs, load_sem,
):
    me = lax.axis_index("hilbert")
    owner = hosted_by(me)
    my_host = host_of(me)
    near = [lax.rem(me + o, N) for o in OFFS]
    hosts = [host_of(p) for p in near]
    holders = [lax.rem(owner + o, N) for o in OFFS]
    peers = [host_of(p) for p in holders]
    stages = []
    for stride, size in ((1, 2), (2, 4), (8, 4), (32, 4)):
        digit = lax.rem(me // stride, size)
        stages.append(
            [(me + (lax.rem(digit + j, size) - digit) * stride, size - 1 - j) for j in range(1, size)]
        )
    first_sum = (0, 1, 4, 7)

    barrier = pltpu.get_barrier_semaphore()
    partners = peers + hosts + holders + [my_host, owner] + [p for stage in stages for p, _ in stage]
    for p in partners:
        pl.semaphore_signal(barrier, inc=1, device_id=(p,), device_id_type=pl.DeviceIdType.MESH)

    loads = [
        pltpu.make_async_copy(mass_hbm, mass_ref, load_sem.at[0]),
        pltpu.make_async_copy(pos_hbm, pos_ref, load_sem.at[1]),
    ]
    for copy in loads:
        copy.start()

    def send(src, dst, ss, rs, p):
        copy = pltpu.make_async_remote_copy(
            src_ref=src, dst_ref=dst, send_sem=ss, recv_sem=rs,
            device_id=(p,), device_id_type=pl.DeviceIdType.MESH,
        )
        copy.start()
        return copy

    def send_lanes(src, dst, ss, rs, to):
        return [
            send(
                src.at[pl.ds(16 * l, 16)], dst.at[pl.ds(16 * BACK[l], 16)],
                ss.at[l], rs.at[BACK[l]], to[l],
            )
            for l in LANE_ORDER
        ]

    lane128 = iota((1, 128), 1)
    offs_row = jnp.where(
        lane128 < 4,
        lane128 + 1,
        jnp.where(lane128 < 8, 131 - lane128, jnp.where(lane128 == 8, 64, -1)),
    )
    lane_f = lane128.astype(f32)

    def slots_of(match):
        rows = match.shape[0]
        earlier = (iota((rows, rows), 0) > iota((rows, rows), 1)).astype(f32).astype(bf16)
        rank = jnp.sum(dot(earlier, match.astype(bf16)) * match, axis=1, keepdims=True)
        lane = jnp.sum(match * lane_f, axis=1, keepdims=True)
        away = jnp.sum(match, axis=1, keepdims=True)
        return jnp.where(away > 0.5, lane * 16.0 + rank, -1000.0)

    def face_slots(columns, of):
        delta = (columns[0:O, 0:6] - of + N) % N
        match = jnp.concatenate(
            [(delta[:, f : f + 1] == offs_row).astype(f32) for f in range(6)], axis=0
        )
        return (slots_of(match) == iota((F6, ROWS), 1).astype(f32)).astype(f32)

    def set_tables(role, columns, of):
        group = iota((O, F6), 1) // S
        inside = iota((O, F6), 1) % S

        def spread(base):
            total = jnp.zeros((O, F6), i32)
            for f in range(6):
                total = jnp.where(group == f, columns[0:O, base + f : base + f + 1], total)
            return total

        takes = face_slots(columns, of)
        gro = takes[0:O]
        for f in range(1, 6):
            gro = gro + takes[f * O : (f + 1) * O]
        gro_ref[role] = gro.astype(bf16)
        same_face = (iota((F6, F6), 0) // O == iota((F6, F6), 1) // S).astype(f32).astype(bf16)
        smask_ref[role] = dot_t(takes.astype(bf16), same_face).astype(bf16)
        home_ref[role] = ((spread(0) == of) & (spread(8) == inside)).astype(f32).astype(bf16)
        coarse_x = spread(16)
        quad_x = spread(24)
        quad_in = (inside // 32) * 2 + (inside % 8) // 4
        m0 = (coarse_x != 1).astype(f32).astype(bf16)
        mc = ((coarse_x == 1) & (quad_x == quad_in)).astype(f32).astype(bf16)
        m0_ref[role] = jnp.concatenate([m0, m0], axis=0)
        mc_ref[role] = jnp.concatenate([mc, mc], axis=0)

    index_ref[...] = jnp.zeros((128, 128), f32)
    for f in range(6):
        index_ref[f : f + 1, 0:O] = fown_ref[f].astype(f32)
        index_ref[8 + f : 9 + f, 0:O] = foct_ref[f : f + 1].astype(f32)
        index_ref[16 + f : 17 + f, 0:O] = fco_ref[f : f + 1].astype(f32)
        index_ref[24 + f : 25 + f, 0:O] = fq_ref[f : f + 1].astype(f32)
    index_ref[32:33, :] = bown_ref[...].astype(f32)
    index_ref[33:34, :] = boct_ref[...].astype(f32)
    columns = index_ref[...].T.astype(i32)

    takes = face_slots(columns, me)
    oct_col = jnp.concatenate([columns[0:O, 8 + f : 9 + f] for f in range(6)], axis=0)
    lane_wide = iota((F6, 128), 1)
    row_face = iota((F6, 128), 0) // O
    wanted = jnp.where(
        lane_wide < S, (oct_col == lane_wide).astype(f32), (lane_wide - S == row_face).astype(f32)
    ).astype(bf16)

    block_delta = (columns[:, 32:33] - me + N) % N
    block_slot = slots_of((block_delta == offs_row).astype(f32))
    slot_lane = iota((B, ROWS), 1).astype(f32)
    into = [(block_slot + 4.0 * d == slot_lane).astype(f32).astype(bf16) for d in range(3)]
    oct_is = columns[:, 33:34] == iota((B, 128), 1)
    at_home = ((block_delta == 0) & oct_is).astype(f32).astype(bf16)
    oct_hot = oct_is.astype(f32).astype(bf16)
    req_send[:, 0:128] = dot_t(takes.astype(bf16), wanted).astype(bf16)
    req_send[:, 128:256] = dot_t(into[0] + into[1] + into[2], oct_hot).astype(bf16)

    for copy in loads:
        copy.wait()
    masses = mass_ref[...]
    tile = masses[0:8, 0:128]
    for r in range(16):
        for h in range(2):
            if r or h:
                tile = tile + masses[8 * r : 8 * r + 8, 128 * h : 128 * h + 128]

    def deposit(i, carry):
        rows = pl.ds(pl.multiple_of(i * 32, 32), 32)
        xs, ys, zs, ms = pos_ref[0, rows, :], pos_ref[1, rows, :], pos_ref[2, rows, :], mass_ref[rows, :]
        for r in range(32):
            wx = weights(xs[r : r + 1]) * ms[r : r + 1]
            high, low = crossed(weights(ys[r : r + 1]), weights(zs[r : r + 1]))
            x_high = wx.astype(bf16).astype(f32)
            left = jnp.concatenate([x_high, wx - x_high], axis=0).astype(bf16)
            right = jnp.concatenate([high, low], axis=0)
            both = lax.dot_general(
                left, right, (((1,), (1,)), ((), ())), preferred_element_type=f32
            )
            dep_ref[pl.ds(pl.multiple_of(i * 256 + 8 * r, 8), 8), :] = both[0:8] + both[8:16]
            cross_ref[pl.ds(pl.multiple_of(i * 4096 + 128 * r, 128), 128), :] = right
        return carry

    lax.fori_loop(0, B // 64, deposit, 0)

    pl.semaphore_wait(barrier, len(partners))

    requests = send_lanes(req_send, req_got, req_ss, req_rs, hosts)
    index_copy = send(index_ref.at[pl.ds(0, 32)], index_got, one_ss.at[0], one_rs.at[0], my_host)
    sums = []

    def sum_start(s, tile):
        sum_send[s] = tile
        for j, (p, back) in enumerate(stages[s]):
            at = first_sum[s]
            sums.append(
                send(sum_send.at[s], sum_got.at[at + back], sum_ss.at[at + j], sum_rs.at[at + back], p)
            )

    def sum_end(s, tile):
        at, count = first_sum[s], len(stages[s])
        for copy in sums[at : at + count]:
            copy.wait_recv()
        for j in range(count):
            tile = tile + sum_got[at + j]
        return tile

    sum_start(0, tile)

    lax.fori_loop(B // 64, B // 32, deposit, 0)

    low_half = iota((B, 128), 1) < S
    parts = []
    for i in range(4):
        even = dep_ref[pl.ds(2 * i, B, stride=8), :]
        odd = dep_ref[pl.ds(2 * i + 1, B, stride=8), :]
        parts.append(
            jnp.where(low_half, even + pltpu.roll(even, S, 1), odd + pltpu.roll(odd, S, 1))
        )
    rest = jnp.concatenate(parts, axis=1)
    pieces = []
    for _ in range(3):
        piece = rest.astype(bf16)
        rest = rest - piece.astype(f32)
        pieces.append(piece)
    stacked = jnp.concatenate(pieces, axis=0)
    msg_send[...] = dot_t(jnp.concatenate(into, axis=0), stacked).astype(bf16)
    deposits = send_lanes(msg_send, dep_got, msg_ss, dep_rs, hosts)
    home = dot_t(jnp.concatenate([at_home] * 3, axis=0), stacked)[0:O]
    home_send[...] = home.astype(bf16)
    home_copy = send(home_send, home_got, one_ss.at[1], one_rs.at[1], my_host)
    homelo_send[...] = (home - home.astype(bf16).astype(f32)).astype(bf16)
    homelo_copy = send(homelo_send, homelo_got, one_ss.at[4], one_rs.at[4], my_host)

    for d in range(3):
        pick_ref[:, 128 * d : 128 * d + 128] = pick_table(d)
        place_ref[256 * d : 256 * d + 256, :] = place_table(d)
    for d in range(3):
        rows = slice(256 * d, 256 * d + 256)
        next_ref[rows, :] = dot(place_ref[rows, :], pick_ref[...]).astype(bf16)
    diag_ref[...] = (iota((F6, F6), 0) // S == iota((F6, F6), 1) // S).astype(f32).astype(bf16)
    to_face = (iota((128, F6), 0) - S == iota((128, F6), 1) // S).astype(f32).astype(bf16)

    tile = sum_end(0, tile)
    sum_start(1, tile)

    index_copy.wait_recv()
    spare = jnp.zeros((96, 128), f32)
    columns = jnp.concatenate([index_got[...], spare], axis=0).T.astype(i32)
    set_tables(0, columns, owner)

    for copy in requests:
        copy.wait_recv()
    asks = req_got[...]
    os_ref[...] = asks[:, 0:S]
    fmask_ref[...] = dot(asks[:, 0:128], to_face)
    slot_octs = asks[:, 128 : 128 + S]

    for copy in deposits:
        copy.wait_recv()
    density = dot_t(slot_octs, dep_got[...])
    home_copy.wait_recv()
    source = COUPLING * (density + home_got[...].astype(f32))
    dens_ref[...] = source
    work_ref[...] = source * (-1.0 / 6.0)

    lane = iota((1, C), 1)
    at = (lane // 64, lane // 8 % 8, lane % 8)
    strides = (64, 8, 1)

    def inner(phi, d):
        up = jnp.where(at[d] < 7, pltpu.roll(phi, C - strides[d], 1), 0.0)
        down = jnp.where(at[d] > 0, pltpu.roll(phi, strides[d], 1), 0.0)
        return up, down

    def placed(raw, d, sign=None, role=0):
        rows = raw.shape[0]
        part = raw[:, 128 * d : 128 * d + 128]
        if sign is not None:
            part = part * sign
        left = jnp.concatenate(
            [
                part * m0_ref[role, 0:rows, 128 * d : 128 * d + 128],
                part * mc_ref[role, 0:rows, 128 * d : 128 * d + 128],
            ],
            axis=1,
        )
        return dot(left, place_ref[256 * d : 256 * d + 256, :])

    def face_copies(slot):
        return [
            pltpu.make_async_remote_copy(
                src_ref=face_send.at[pl.ds(16 * l, 16)],
                dst_ref=face_got.at[slot, pl.ds(16 * BACK[l], 16)],
                send_sem=face_ss.at[l], recv_sem=face_rs.at[slot, BACK[l]],
                device_id=(peers[l],), device_id_type=pl.DeviceIdType.MESH,
            )
            for l in LANE_ORDER
        ]

    def send_faces(chosen, slot):
        chosen = chosen * fmask_ref[...]
        out = chosen[:, 0:128] + chosen[:, 128:256] + chosen[:, 256:384]
        face_send[...] = (out + pltpu.roll(out, S, 1)).astype(bf16)
        for copy in face_copies(slot):
            copy.start()

    def layers_of(values):
        high = values.astype(bf16)
        low = (values - high.astype(f32)).astype(bf16)
        return [dot(x, pick_ref[...]).astype(bf16) for x in (high, low)]

    def home_ghosts(layers, role=0):
        diag = diag_ref[...]
        wide = [jnp.concatenate([x] * 6, axis=0) * diag for x in layers]
        return jnp.concatenate([dot(home_ref[role], x).astype(bf16) for x in wide], axis=0)

    def both_masks(part, d, fine, coarse):
        cols = slice(128 * d, 128 * d + 128)
        return jnp.concatenate([part * fine[:, cols], part * coarse[:, cols]], axis=1)

    def away_ghosts(got, role=0):
        wide = jnp.concatenate([got] * 3, axis=1) * smask_ref[role]
        return dot(gro_ref[role], wide).astype(bf16)

    def sweep(slot, later_slot, between, shift=None):
        between()
        phi = work_ref[...]
        raw = home_ghosts(layers_of(phi))
        total = placed(raw, 0) + placed(raw, 1) + placed(raw, 2)
        total = total[0:O] + total[O : 2 * O] - dens_ref[...]
        for d in range(3):
            up, down = inner(phi, d)
            total = total + (up + down)
        parts = layers_of(total)
        chosen = dot(os_ref[...], parts[0]) + dot(os_ref[...], parts[1])
        copies = face_copies(slot)
        for copy in copies:
            copy.wait_recv()
        got = face_got[slot]
        wide = jnp.concatenate([got] * 3, axis=1) * smask_ref[0]
        raw = dot(slots_ref[...], wide).astype(bf16)
        for d in range(3):
            left = both_masks(raw[:, 128 * d : 128 * d + 128], d, m0s_ref, mcs_ref)
            chosen = chosen + dot(left, next_ref[256 * d : 256 * d + 256, :])
        chosen = chosen * (1.0 / 6.0)
        if shift is not None:
            chosen = chosen + shift()
        for copy in copies:
            copy.wait_send()
        send_faces(chosen, later_slot)
        raw = away_ghosts(got)
        total = total + (placed(raw, 0) + placed(raw, 1) + placed(raw, 2))
        work_ref[...] = total * (1.0 / 6.0)

    tiles = [tile]

    def step_sum(s):
        tiles.append(sum_end(s, tiles[-1]))
        if s < 3:
            sum_start(s + 1, tiles[-1])

    def mean_of_all():
        total = jnp.sum(jnp.sum(tiles[-1], axis=0, keepdims=True), axis=1, keepdims=True)
        return total * (COUPLING / TOTAL_CELLS)

    def add_low():
        homelo_copy.wait_recv()
        low = COUPLING * homelo_got[...].astype(f32)
        dens_ref[...] = dens_ref[...] + low
        work_ref[...] = work_ref[...] - low * (1.0 / 6.0)
        step_sum(1)
        slots_ref[...] = dot(os_ref[...], gro_ref[0]).astype(bf16)
        m0s_ref[...] = dot(os_ref[...], m0_ref[0, 0:O, :]).astype(bf16)
        mcs_ref[...] = dot(os_ref[...], mc_ref[0, 0:O, :]).astype(bf16)

    first = work_ref[...].astype(bf16)
    send_faces(dot(os_ref[...], dot(first, pick_ref[...]).astype(bf16)), 1)
    sweep(1, 2, add_low)
    def own_tables():
        step_sum(2)
        set_tables(1, index_ref[...].T.astype(i32), me)

    sweep(2, 0, own_tables)
    sweep(0, 1, lambda: step_sum(3), lambda: mean_of_all() * (4.0 / 6.0))
    mean = mean_of_all()
    work_ref[...] = work_ref[...] + mean * (4.0 / 6.0)
    dens_ref[...] = dens_ref[...] - mean

    def later(k, carry):
        sweep(lax.rem(k, 3), lax.rem(k + 1, 3), lambda: None)
        return carry

    lax.fori_loop(4, 8, later, 0)

    for copy in deposits:
        copy.wait_send()
    phi = work_ref[...]
    phi_copy = send(work_ref, phi_got, one_ss.at[3], one_rs.at[3], owner)
    sign = jnp.where(iota((1, 128), 1) < S, 0.5, -0.5).astype(bf16)

    def near_field(phi, role):
        raw = home_ghosts(layers_of(phi), role)
        parts = []
        for d in range(3):
            up, down = inner(phi, d)
            part = placed(raw, d, sign, role)
            parts.append(0.5 * (down - up) + part[0:O] + part[O : 2 * O])
        return parts

    def whole_field(local, got, role):
        raw = away_ghosts(got, role)
        return [(local[d] + placed(raw, d, sign, role)).astype(bf16) for d in range(3)]

    local = near_field(phi, 0)
    copies = face_copies(2)
    for copy in copies:
        copy.wait_recv()
    layers_copy = send(face_got.at[2], layers_got, one_ss.at[2], one_rs.at[2], owner)
    field = whole_field(local, face_got[2], 0)
    row_dim = iota((ROWS, 1), 0) % 16 // 4
    picked = [dot(slot_octs, field[d]) for d in range(3)]
    msg_send[...] = jnp.where(
        row_dim == 0, picked[0], jnp.where(row_dim == 1, picked[1], picked[2])
    ).astype(bf16)
    returns = send_lanes(msg_send, field_got, msg_ss, field_rs, holders)

    phi_copy.wait_recv()
    own = phi_got[...]
    phi_ref[...] = own
    local = near_field(own, 1)
    layers_copy.wait_recv()
    field = whole_field(local, layers_got[...], 1)
    mine = [dot(at_home[:, 0:O], field[d]) for d in range(3)]
    for copy in returns:
        copy.wait_recv()
    got = field_got[...]
    for d in range(3):
        values = mine[d] + dot(into[d], got)
        for i in range(4):
            pair = values[:, 128 * i : 128 * i + 128]
            turned = pltpu.roll(pair, S, 1)
            field_ref[d, pl.ds(2 * i, B, stride=8), :] = jnp.where(low_half, pair, turned)
            field_ref[d, pl.ds(2 * i + 1, B, stride=8), :] = jnp.where(low_half, turned, pair)

    def interpolate(i, carry):
        rows = pl.ds(pl.multiple_of(i * 32, 32), 32)
        xs = pos_ref[0, rows, :]
        out = [[], [], []]
        for r in range(32):
            wx = weights(xs[r : r + 1])
            both = cross_ref[pl.ds(pl.multiple_of(i * 4096 + 128 * r, 128), 128), :]
            at = pl.ds(pl.multiple_of(i * 256 + 8 * r, 8), 8)
            left = jnp.concatenate([field_ref[d, at, :] for d in range(3)], axis=0).astype(bf16)
            value = dot(left, both)
            for d in range(3):
                out[d].append(jnp.sum(value[8 * d : 8 * d + 8] * wx, axis=0, keepdims=True))
        for d in range(3):
            accel_ref[d, rows, :] = jnp.concatenate(out[d], axis=0)
        return carry

    lax.fori_loop(0, B // 32, interpolate, 0)

    for copy in [index_copy, home_copy, homelo_copy, phi_copy, layers_copy] + requests + sums + copies + returns:
        copy.wait_send()


def on_device(
    positions, masses, block_owner, block_oct, face_owner, face_oct, face_coarse, face_quadrant
):
    dma = pltpu.SemaphoreType.DMA
    vmem = pl.BlockSpec(memory_space=pltpu.VMEM)
    potential, accel = pl.pallas_call(
        kernel,
        out_shape=(
            jax.ShapeDtypeStruct((O, C), f32),
            jax.ShapeDtypeStruct((3, B, PART), f32),
        ),
        in_specs=[pl.BlockSpec(memory_space=pl.ANY)] * 2 + [vmem] * 6,
        out_specs=(vmem, vmem),
        scratch_shapes=[
            pltpu.VMEM((B * 8, 128), f32),
            pltpu.VMEM((ROWS, 256), bf16),
            pltpu.VMEM((ROWS, 256), bf16),
            pltpu.VMEM((ROWS, C), bf16),
            pltpu.VMEM((ROWS, C), bf16),
            pltpu.VMEM((ROWS, C), bf16),
            pltpu.VMEM((ROWS, 128), bf16),
            pltpu.VMEM((3, ROWS, 128), bf16),
            pltpu.VMEM((4, 8, 128), f32),
            pltpu.VMEM((10, 8, 128), f32),
            pltpu.VMEM((3, B * 8, 128), f32),
            pltpu.VMEM((O, C), f32),
            pltpu.VMEM((2, 2 * O, F6), bf16),
            pltpu.VMEM((2, 2 * O, F6), bf16),
            pltpu.VMEM((2, O, F6), bf16),
            pltpu.VMEM((ROWS, F6), f32),
            pltpu.VMEM((2, ROWS, F6), bf16),
            pltpu.VMEM((2, O, ROWS), bf16),
            pltpu.VMEM((ROWS, S), bf16),
            pltpu.VMEM((C, F6), bf16),
            pltpu.VMEM((768, C), bf16),
            pltpu.VMEM((F6, F6), bf16),
            pltpu.VMEM((128, 128), f32),
            pltpu.VMEM((32, 128), f32),
            pltpu.VMEM((O, C), bf16),
            pltpu.VMEM((O, C), bf16),
            pltpu.VMEM((ROWS, 128), bf16),
            pltpu.VMEM((O, C), f32),
            pltpu.VMEM((O, C), f32),
            pltpu.VMEM((3, B, PART), f32),
            pltpu.VMEM((B, PART), f32),
            pltpu.VMEM((B * 128, PART), bf16),
            pltpu.VMEM((O, C), bf16),
            pltpu.VMEM((O, C), bf16),
            pltpu.VMEM((ROWS, ROWS), bf16),
            pltpu.VMEM((ROWS, F6), bf16),
            pltpu.VMEM((ROWS, F6), bf16),
            pltpu.VMEM((768, F6), bf16),
            dma((LANES,)),
            dma((LANES,)),
            dma((LANES,)),
            dma((LANES,)),
            dma((LANES,)),
            dma((LANES,)),
            dma((3, LANES)),
            dma((10,)),
            dma((10,)),
            dma((5,)),
            dma((5,)),
            dma((2,)),
        ],
        compiler_params=pltpu.CompilerParams(
            collective_id=0, has_side_effects=True, vmem_limit_bytes=54528 * 1024
        ),
    )(
        jnp.transpose(positions, (1, 0, 2)),
        masses,
        block_owner.T,
        block_oct[None, :],
        jnp.transpose(face_owner, (1, 2, 0)),
        face_oct.T,
        face_coarse.T,
        face_quadrant.T,
    )
    return potential, jnp.transpose(accel, (1, 0, 2))


def solution(mesh):
    placed = (
        P("hilbert", None, None),
        P("hilbert", None),
        P("hilbert", None),
        P("hilbert"),
        P("hilbert", None, None),
        P("hilbert", None),
        P("hilbert", None),
        P("hilbert", None),
    )
    return jax.shard_map(
        on_device,
        mesh=mesh,
        in_specs=placed,
        out_specs=(P("hilbert", None), P("hilbert", None, None)),
        check_vma=False,
    )
```

```python
import jax
import jax.numpy as jnp
from jax import lax
from jax.experimental import pallas as pl
from jax.experimental.pallas import tpu as pltpu
from jax.sharding import PartitionSpec as P

N = 128
B = 128
O = 64
C = 512
S = 64
F6 = 6 * S
PART = 256
OFFS = (1, 2, 3, 4, 127, 126, 125, 124, 64)
BACK = (4, 5, 6, 7, 0, 1, 2, 3, 8)
LANES = len(OFFS)
LANE_ORDER = (3, 7, 2, 6, 8, 1, 5, 0, 4)
ROWS = 16 * LANES
TOTAL_CELLS = float(N * O * C)
COUPLING = 0.25

f32 = jnp.float32
bf16 = jnp.bfloat16
i32 = jnp.int32


def dot(a, b):
    return jnp.dot(a, b, preferred_element_type=f32)


def dot_t(a, b):
    return lax.dot_general(a, b, (((0,), (0,)), ((), ())), preferred_element_type=f32)


def iota(shape, dim):
    return lax.broadcasted_iota(i32, shape, dim)


def pick_table(d):
    cell, lane = iota((C, 128), 0), iota((C, 128), 1)
    coord, spot = cell_spot(cell, d)
    return ((coord == jnp.where(lane < S, 7, 0)) & (spot == lane % S)).astype(f32).astype(bf16)


def place_table(d):
    row, cell = iota((256, C), 0), iota((256, C), 1)
    coord, spot = cell_spot(cell, d)
    j = row % S
    here = coord == (row // S % 2) * 7
    fine = spot == j
    coarse = ((spot // 16) == (j // 8 % 4)) & ((spot % 8) // 2 == j % 4)
    return (here & (((row < 128) & fine) | ((row >= 128) & coarse))).astype(f32).astype(bf16)


def cell_spot(cell, d):
    x, y, z = cell // 64, cell // 8 % 8, cell % 8
    return ((x, y * 8 + z), (y, x * 8 + z), (z, x * 8 + y))[d]


def weights(row):
    centres = iota((8, PART), 0).astype(f32) + 0.5
    return jnp.maximum(0.0, 1.0 - jnp.abs(row - centres))


def crossed(wy, wz):
    full = jnp.concatenate([wy[y : y + 1] * wz for y in range(8)], axis=0)
    high = full.astype(bf16)
    return high, (full - high.astype(f32)).astype(bf16)


def device_at(x, z, y, core):
    return x * 32 + z * 8 + y * 2 + core


def host_of(i):
    x, z, y = i // 32, lax.rem(i // 8, 4), lax.rem(i // 2, 4)
    return device_at(
        lax.rem(x + 3, 4),
        z + lax.rem(x, 2) * (3 - 2 * z),
        y + lax.rem(z, 2) * (3 - 2 * y),
        lax.rem(i, 2),
    )


def hosted_by(i):
    x, z, y = lax.rem(i // 32 + 1, 4), lax.rem(i // 8, 4), lax.rem(i // 2, 4)
    z = z + lax.rem(x, 2) * (3 - 2 * z)
    return device_at(x, z, y + lax.rem(z, 2) * (3 - 2 * y), lax.rem(i, 2))


def kernel(
    pos_hbm, mass_hbm, bown_ref, boct_ref, fown_ref, foct_ref, fco_ref, fq_ref,
    phi_ref, accel_ref,
    dep_ref, req_send, req_got, msg_send, dep_got, field_got, face_send, face_got,
    sum_send, sum_got, field_ref, dens_ref, m0_ref, mc_ref, home_ref, fmask_ref, smask_ref, gro_ref, os_ref,
    pick_ref, place_ref, diag_ref, index_ref, index_got, home_send, home_got, layers_got,
    work_ref, phi_got, pos_ref, mass_ref, cross_ref, homelo_send, homelo_got,
    slots_ref, m0s_ref, mcs_ref, next_ref,
    req_ss, req_rs, msg_ss, dep_rs, field_rs, face_ss, face_rs, sum_ss, sum_rs, one_ss, one_rs, load_sem,
):
    me = lax.axis_index("hilbert")
    owner = hosted_by(me)
    my_host = host_of(me)
    near = [lax.rem(me + o, N) for o in OFFS]
    hosts = [host_of(p) for p in near]
    holders = [lax.rem(owner + o, N) for o in OFFS]
    peers = [host_of(p) for p in holders]
    stages = []
    for stride, size in ((1, 2), (2, 4), (8, 4), (32, 4)):
        digit = lax.rem(me // stride, size)
        stages.append(
            [(me + (lax.rem(digit + j, size) - digit) * stride, size - 1 - j) for j in range(1, size)]
        )
    first_sum = (0, 1, 4, 7)

    barrier = pltpu.get_barrier_semaphore()
    partners = peers + hosts + holders + [my_host, owner] + [p for stage in stages for p, _ in stage]
    for p in partners:
        pl.semaphore_signal(barrier, inc=1, device_id=(p,), device_id_type=pl.DeviceIdType.MESH)

    loads = [
        pltpu.make_async_copy(mass_hbm, mass_ref, load_sem.at[0]),
        pltpu.make_async_copy(pos_hbm, pos_ref, load_sem.at[1]),
    ]
    for copy in loads:
        copy.start()

    def send(src, dst, ss, rs, p):
        copy = pltpu.make_async_remote_copy(
            src_ref=src, dst_ref=dst, send_sem=ss, recv_sem=rs,
            device_id=(p,), device_id_type=pl.DeviceIdType.MESH,
        )
        copy.start()
        return copy

    def send_lanes(src, dst, ss, rs, to):
        return [
            send(
                src.at[pl.ds(16 * l, 16)], dst.at[pl.ds(16 * BACK[l], 16)],
                ss.at[l], rs.at[BACK[l]], to[l],
            )
            for l in LANE_ORDER
        ]

    lane128 = iota((1, 128), 1)
    offs_row = jnp.where(
        lane128 < 4,
        lane128 + 1,
        jnp.where(lane128 < 8, 131 - lane128, jnp.where(lane128 == 8, 64, -1)),
    )
    lane_f = lane128.astype(f32)

    def slots_of(match):
        rows = match.shape[0]
        earlier = (iota((rows, rows), 0) > iota((rows, rows), 1)).astype(f32).astype(bf16)
        rank = jnp.sum(dot(earlier, match.astype(bf16)) * match, axis=1, keepdims=True)
        lane = jnp.sum(match * lane_f, axis=1, keepdims=True)
        away = jnp.sum(match, axis=1, keepdims=True)
        return jnp.where(away > 0.5, lane * 16.0 + rank, -1000.0)

    def face_slots(columns, of):
        delta = (columns[0:O, 0:6] - of + N) % N
        match = jnp.concatenate(
            [(delta[:, f : f + 1] == offs_row).astype(f32) for f in range(6)], axis=0
        )
        return (slots_of(match) == iota((F6, ROWS), 1).astype(f32)).astype(f32)

    def set_tables(role, columns, of):
        group = iota((O, F6), 1) // S
        inside = iota((O, F6), 1) % S

        def spread(base):
            total = jnp.zeros((O, F6), i32)
            for f in range(6):
                total = jnp.where(group == f, columns[0:O, base + f : base + f + 1], total)
            return total

        takes = face_slots(columns, of)
        gro = takes[0:O]
        for f in range(1, 6):
            gro = gro + takes[f * O : (f + 1) * O]
        gro_ref[role] = gro.astype(bf16)
        same_face = (iota((F6, F6), 0) // O == iota((F6, F6), 1) // S).astype(f32).astype(bf16)
        smask_ref[role] = dot_t(takes.astype(bf16), same_face).astype(bf16)
        home_ref[role] = ((spread(0) == of) & (spread(8) == inside)).astype(f32).astype(bf16)
        coarse_x = spread(16)
        quad_x = spread(24)
        quad_in = (inside // 32) * 2 + (inside % 8) // 4
        m0 = (coarse_x != 1).astype(f32).astype(bf16)
        mc = ((coarse_x == 1) & (quad_x == quad_in)).astype(f32).astype(bf16)
        m0_ref[role] = jnp.concatenate([m0, m0], axis=0)
        mc_ref[role] = jnp.concatenate([mc, mc], axis=0)

    index_ref[...] = jnp.zeros((128, 128), f32)
    for f in range(6):
        index_ref[f : f + 1, 0:O] = fown_ref[f].astype(f32)
        index_ref[8 + f : 9 + f, 0:O] = foct_ref[f : f + 1].astype(f32)
        index_ref[16 + f : 17 + f, 0:O] = fco_ref[f : f + 1].astype(f32)
        index_ref[24 + f : 25 + f, 0:O] = fq_ref[f : f + 1].astype(f32)
    index_ref[32:33, :] = bown_ref[...].astype(f32)
    index_ref[33:34, :] = boct_ref[...].astype(f32)
    columns = index_ref[...].T.astype(i32)

    takes = face_slots(columns, me)
    oct_col = jnp.concatenate([columns[0:O, 8 + f : 9 + f] for f in range(6)], axis=0)
    lane_wide = iota((F6, 128), 1)
    row_face = iota((F6, 128), 0) // O
    wanted = jnp.where(
        lane_wide < S, (oct_col == lane_wide).astype(f32), (lane_wide - S == row_face).astype(f32)
    ).astype(bf16)

    block_delta = (columns[:, 32:33] - me + N) % N
    block_slot = slots_of((block_delta == offs_row).astype(f32))
    slot_lane = iota((B, ROWS), 1).astype(f32)
    into = [(block_slot + 4.0 * d == slot_lane).astype(f32).astype(bf16) for d in range(3)]
    oct_is = columns[:, 33:34] == iota((B, 128), 1)
    at_home = ((block_delta == 0) & oct_is).astype(f32).astype(bf16)
    oct_hot = oct_is.astype(f32).astype(bf16)
    req_send[:, 0:128] = dot_t(takes.astype(bf16), wanted).astype(bf16)
    req_send[:, 128:256] = dot_t(into[0] + into[1] + into[2], oct_hot).astype(bf16)

    for copy in loads:
        copy.wait()
    masses = mass_ref[...]
    tile = masses[0:8, 0:128]
    for r in range(16):
        for h in range(2):
            if r or h:
                tile = tile + masses[8 * r : 8 * r + 8, 128 * h : 128 * h + 128]

    def deposit(i, carry):
        rows = pl.ds(pl.multiple_of(i * 32, 32), 32)
        xs, ys, zs, ms = pos_ref[0, rows, :], pos_ref[1, rows, :], pos_ref[2, rows, :], mass_ref[rows, :]
        for r in range(32):
            wx = weights(xs[r : r + 1]) * ms[r : r + 1]
            high, low = crossed(weights(ys[r : r + 1]), weights(zs[r : r + 1]))
            x_high = wx.astype(bf16).astype(f32)
            left = jnp.concatenate([x_high, wx - x_high], axis=0).astype(bf16)
            right = jnp.concatenate([high, low], axis=0)
            both = lax.dot_general(
                left, right, (((1,), (1,)), ((), ())), preferred_element_type=f32
            )
            dep_ref[pl.ds(pl.multiple_of(i * 256 + 8 * r, 8), 8), :] = both[0:8] + both[8:16]
            cross_ref[pl.ds(pl.multiple_of(i * 4096 + 128 * r, 128), 128), :] = right
        return carry

    lax.fori_loop(0, B // 64, deposit, 0)

    pl.semaphore_wait(barrier, len(partners))

    requests = send_lanes(req_send, req_got, req_ss, req_rs, hosts)
    index_copy = send(index_ref.at[pl.ds(0, 32)], index_got, one_ss.at[0], one_rs.at[0], my_host)
    sums = []

    def sum_start(s, tile):
        sum_send[s] = tile
        for j, (p, back) in enumerate(stages[s]):
            at = first_sum[s]
            sums.append(
                send(sum_send.at[s], sum_got.at[at + back], sum_ss.at[at + j], sum_rs.at[at + back], p)
            )

    def sum_end(s, tile):
        at, count = first_sum[s], len(stages[s])
        for copy in sums[at : at + count]:
            copy.wait_recv()
        for j in range(count):
            tile = tile + sum_got[at + j]
        return tile

    sum_start(0, tile)

    lax.fori_loop(B // 64, B // 32, deposit, 0)

    low_half = iota((B, 128), 1) < S
    parts = []
    for i in range(4):
        even = dep_ref[pl.ds(2 * i, B, stride=8), :]
        odd = dep_ref[pl.ds(2 * i + 1, B, stride=8), :]
        parts.append(
            jnp.where(low_half, even + pltpu.roll(even, S, 1), odd + pltpu.roll(odd, S, 1))
        )
    rest = jnp.concatenate(parts, axis=1)
    pieces = []
    for _ in range(3):
        piece = rest.astype(bf16)
        rest = rest - piece.astype(f32)
        pieces.append(piece)
    stacked = jnp.concatenate(pieces, axis=0)
    msg_send[...] = dot_t(jnp.concatenate(into, axis=0), stacked).astype(bf16)
    deposits = send_lanes(msg_send, dep_got, msg_ss, dep_rs, hosts)
    home = dot_t(jnp.concatenate([at_home] * 3, axis=0), stacked)[0:O]
    home_send[...] = home.astype(bf16)
    home_copy = send(home_send, home_got, one_ss.at[1], one_rs.at[1], my_host)
    homelo_send[...] = (home - home.astype(bf16).astype(f32)).astype(bf16)
    homelo_copy = send(homelo_send, homelo_got, one_ss.at[4], one_rs.at[4], my_host)

    for d in range(3):
        pick_ref[:, 128 * d : 128 * d + 128] = pick_table(d)
        place_ref[256 * d : 256 * d + 256, :] = place_table(d)
    for d in range(3):
        rows = slice(256 * d, 256 * d + 256)
        next_ref[rows, :] = dot(place_ref[rows, :], pick_ref[...]).astype(bf16)
    diag_ref[...] = (iota((F6, F6), 0) // S == iota((F6, F6), 1) // S).astype(f32).astype(bf16)
    to_face = (iota((128, F6), 0) - S == iota((128, F6), 1) // S).astype(f32).astype(bf16)

    tile = sum_end(0, tile)
    sum_start(1, tile)

    index_copy.wait_recv()
    spare = jnp.zeros((96, 128), f32)
    columns = jnp.concatenate([index_got[...], spare], axis=0).T.astype(i32)
    set_tables(0, columns, owner)

    for copy in requests:
        copy.wait_recv()
    asks = req_got[...]
    os_ref[...] = asks[:, 0:S]
    fmask_ref[...] = dot(asks[:, 0:128], to_face)
    slot_octs = asks[:, 128 : 128 + S]

    for copy in deposits:
        copy.wait_recv()
    density = dot_t(slot_octs, dep_got[...])
    home_copy.wait_recv()
    source = COUPLING * (density + home_got[...].astype(f32))
    dens_ref[...] = source
    work_ref[...] = source * (-1.0 / 6.0)

    lane = iota((1, C), 1)
    at = (lane // 64, lane // 8 % 8, lane % 8)
    strides = (64, 8, 1)

    def inner(phi, d):
        up = jnp.where(at[d] < 7, pltpu.roll(phi, C - strides[d], 1), 0.0)
        down = jnp.where(at[d] > 0, pltpu.roll(phi, strides[d], 1), 0.0)
        return up, down

    def placed(raw, d, sign=None, role=0):
        rows = raw.shape[0]
        part = raw[:, 128 * d : 128 * d + 128]
        if sign is not None:
            part = part * sign
        left = jnp.concatenate(
            [
                part * m0_ref[role, 0:rows, 128 * d : 128 * d + 128],
                part * mc_ref[role, 0:rows, 128 * d : 128 * d + 128],
            ],
            axis=1,
        )
        return dot(left, place_ref[256 * d : 256 * d + 256, :])

    def face_copies(slot):
        return [
            pltpu.make_async_remote_copy(
                src_ref=face_send.at[pl.ds(16 * l, 16)],
                dst_ref=face_got.at[slot, pl.ds(16 * BACK[l], 16)],
                send_sem=face_ss.at[l], recv_sem=face_rs.at[slot, BACK[l]],
                device_id=(peers[l],), device_id_type=pl.DeviceIdType.MESH,
            )
            for l in LANE_ORDER
        ]

    def send_faces(chosen, slot):
        chosen = chosen * fmask_ref[...]
        out = chosen[:, 0:128] + chosen[:, 128:256] + chosen[:, 256:384]
        face_send[...] = (out + pltpu.roll(out, S, 1)).astype(bf16)
        for copy in face_copies(slot):
            copy.start()

    def layers_of(values):
        high = values.astype(bf16)
        low = (values - high.astype(f32)).astype(bf16)
        return [dot(x, pick_ref[...]).astype(bf16) for x in (high, low)]

    def home_ghosts(layers, role=0):
        diag = diag_ref[...]
        wide = [jnp.concatenate([x] * 6, axis=0) * diag for x in layers]
        return jnp.concatenate([dot(home_ref[role], x).astype(bf16) for x in wide], axis=0)

    def both_masks(part, d, fine, coarse):
        cols = slice(128 * d, 128 * d + 128)
        return jnp.concatenate([part * fine[:, cols], part * coarse[:, cols]], axis=1)

    def away_ghosts(got, role=0):
        wide = jnp.concatenate([got] * 3, axis=1) * smask_ref[role]
        return dot(gro_ref[role], wide).astype(bf16)

    def sweep(slot, later_slot, between, shift=None):
        between()
        phi = work_ref[...]
        raw = home_ghosts(layers_of(phi))
        total = placed(raw, 0) + placed(raw, 1) + placed(raw, 2)
        total = total[0:O] + total[O : 2 * O] - dens_ref[...]
        for d in range(3):
            up, down = inner(phi, d)
            total = total + (up + down)
        parts = layers_of(total)
        chosen = dot(os_ref[...], parts[0]) + dot(os_ref[...], parts[1])
        copies = face_copies(slot)
        for copy in copies:
            copy.wait_send()
        for copy in copies:
            copy.wait_recv()
        got = face_got[slot]
        wide = jnp.concatenate([got] * 3, axis=1) * smask_ref[0]
        raw = dot(slots_ref[...], wide).astype(bf16)
        for d in range(3):
            left = both_masks(raw[:, 128 * d : 128 * d + 128], d, m0s_ref, mcs_ref)
            chosen = chosen + dot(left, next_ref[256 * d : 256 * d + 256, :])
        chosen = chosen * (1.0 / 6.0)
        if shift is not None:
            chosen = chosen + shift()
        send_faces(chosen, later_slot)
        raw = away_ghosts(got)
        total = total + (placed(raw, 0) + placed(raw, 1) + placed(raw, 2))
        work_ref[...] = total * (1.0 / 6.0)

    tiles = [tile]

    def step_sum(s):
        tiles.append(sum_end(s, tiles[-1]))
        if s < 3:
            sum_start(s + 1, tiles[-1])

    def mean_of_all():
        total = jnp.sum(jnp.sum(tiles[-1], axis=0, keepdims=True), axis=1, keepdims=True)
        return total * (COUPLING / TOTAL_CELLS)

    def add_low():
        homelo_copy.wait_recv()
        low = COUPLING * homelo_got[...].astype(f32)
        dens_ref[...] = dens_ref[...] + low
        work_ref[...] = work_ref[...] - low * (1.0 / 6.0)
        step_sum(1)
        slots_ref[...] = dot(os_ref[...], gro_ref[0]).astype(bf16)
        m0s_ref[...] = dot(os_ref[...], m0_ref[0, 0:O, :]).astype(bf16)
        mcs_ref[...] = dot(os_ref[...], mc_ref[0, 0:O, :]).astype(bf16)

    first = work_ref[...].astype(bf16)
    send_faces(dot(os_ref[...], dot(first, pick_ref[...]).astype(bf16)), 1)
    sweep(1, 2, add_low)
    def own_tables():
        step_sum(2)
        set_tables(1, index_ref[...].T.astype(i32), me)

    sweep(2, 0, own_tables)
    sweep(0, 1, lambda: step_sum(3), lambda: mean_of_all() * (4.0 / 6.0))
    mean = mean_of_all()
    work_ref[...] = work_ref[...] + mean * (4.0 / 6.0)
    dens_ref[...] = dens_ref[...] - mean

    def later(k, carry):
        sweep(lax.rem(k, 3), lax.rem(k + 1, 3), lambda: None)
        return carry

    lax.fori_loop(4, 8, later, 0)

    for copy in deposits:
        copy.wait_send()
    phi = work_ref[...]
    phi_copy = send(work_ref, phi_got, one_ss.at[3], one_rs.at[3], owner)
    sign = jnp.where(iota((1, 128), 1) < S, 0.5, -0.5).astype(bf16)

    def near_field(phi, role):
        raw = home_ghosts(layers_of(phi), role)
        parts = []
        for d in range(3):
            up, down = inner(phi, d)
            part = placed(raw, d, sign, role)
            parts.append(0.5 * (down - up) + part[0:O] + part[O : 2 * O])
        return parts

    def whole_field(local, got, role):
        raw = away_ghosts(got, role)
        return [(local[d] + placed(raw, d, sign, role)).astype(bf16) for d in range(3)]

    local = near_field(phi, 0)
    copies = face_copies(2)
    for copy in copies:
        copy.wait_recv()
    layers_copy = send(face_got.at[2], layers_got, one_ss.at[2], one_rs.at[2], owner)
    field = whole_field(local, face_got[2], 0)
    row_dim = iota((ROWS, 1), 0) % 16 // 4
    picked = [dot(slot_octs, field[d]) for d in range(3)]
    msg_send[...] = jnp.where(
        row_dim == 0, picked[0], jnp.where(row_dim == 1, picked[1], picked[2])
    ).astype(bf16)
    returns = send_lanes(msg_send, field_got, msg_ss, field_rs, holders)

    phi_copy.wait_recv()
    own = phi_got[...]
    phi_ref[...] = own
    local = near_field(own, 1)
    layers_copy.wait_recv()
    field = whole_field(local, layers_got[...], 1)
    mine = [dot(at_home[:, 0:O], field[d]) for d in range(3)]
    for copy in returns:
        copy.wait_recv()
    got = field_got[...]
    for d in range(3):
        values = mine[d] + dot(into[d], got)
        for i in range(4):
            pair = values[:, 128 * i : 128 * i + 128]
            turned = pltpu.roll(pair, S, 1)
            field_ref[d, pl.ds(2 * i, B, stride=8), :] = jnp.where(low_half, pair, turned)
            field_ref[d, pl.ds(2 * i + 1, B, stride=8), :] = jnp.where(low_half, turned, pair)

    def interpolate(i, carry):
        rows = pl.ds(pl.multiple_of(i * 32, 32), 32)
        xs = pos_ref[0, rows, :]
        out = [[], [], []]
        for r in range(32):
            wx = weights(xs[r : r + 1])
            both = cross_ref[pl.ds(pl.multiple_of(i * 4096 + 128 * r, 128), 128), :]
            at = pl.ds(pl.multiple_of(i * 256 + 8 * r, 8), 8)
            left = jnp.concatenate([field_ref[d, at, :] for d in range(3)], axis=0).astype(bf16)
            value = dot(left, both)
            for d in range(3):
                out[d].append(jnp.sum(value[8 * d : 8 * d + 8] * wx, axis=0, keepdims=True))
        for d in range(3):
            accel_ref[d, rows, :] = jnp.concatenate(out[d], axis=0)
        return carry

    lax.fori_loop(0, B // 32, interpolate, 0)

    for copy in [index_copy, home_copy, homelo_copy, phi_copy, layers_copy] + requests + sums + copies + returns:
        copy.wait_send()


def on_device(
    positions, masses, block_owner, block_oct, face_owner, face_oct, face_coarse, face_quadrant
):
    dma = pltpu.SemaphoreType.DMA
    vmem = pl.BlockSpec(memory_space=pltpu.VMEM)
    potential, accel = pl.pallas_call(
        kernel,
        out_shape=(
            jax.ShapeDtypeStruct((O, C), f32),
            jax.ShapeDtypeStruct((3, B, PART), f32),
        ),
        in_specs=[pl.BlockSpec(memory_space=pl.ANY)] * 2 + [vmem] * 6,
        out_specs=(vmem, vmem),
        scratch_shapes=[
            pltpu.VMEM((B * 8, 128), f32),
            pltpu.VMEM((ROWS, 256), bf16),
            pltpu.VMEM((ROWS, 256), bf16),
            pltpu.VMEM((ROWS, C), bf16),
            pltpu.VMEM((ROWS, C), bf16),
            pltpu.VMEM((ROWS, C), bf16),
            pltpu.VMEM((ROWS, 128), bf16),
            pltpu.VMEM((3, ROWS, 128), bf16),
            pltpu.VMEM((4, 8, 128), f32),
            pltpu.VMEM((10, 8, 128), f32),
            pltpu.VMEM((3, B * 8, 128), f32),
            pltpu.VMEM((O, C), f32),
            pltpu.VMEM((2, 2 * O, F6), bf16),
            pltpu.VMEM((2, 2 * O, F6), bf16),
            pltpu.VMEM((2, O, F6), bf16),
            pltpu.VMEM((ROWS, F6), f32),
            pltpu.VMEM((2, ROWS, F6), bf16),
            pltpu.VMEM((2, O, ROWS), bf16),
            pltpu.VMEM((ROWS, S), bf16),
            pltpu.VMEM((C, F6), bf16),
            pltpu.VMEM((768, C), bf16),
            pltpu.VMEM((F6, F6), bf16),
            pltpu.VMEM((128, 128), f32),
            pltpu.VMEM((32, 128), f32),
            pltpu.VMEM((O, C), bf16),
            pltpu.VMEM((O, C), bf16),
            pltpu.VMEM((ROWS, 128), bf16),
            pltpu.VMEM((O, C), f32),
            pltpu.VMEM((O, C), f32),
            pltpu.VMEM((3, B, PART), f32),
            pltpu.VMEM((B, PART), f32),
            pltpu.VMEM((B * 128, PART), bf16),
            pltpu.VMEM((O, C), bf16),
            pltpu.VMEM((O, C), bf16),
            pltpu.VMEM((ROWS, ROWS), bf16),
            pltpu.VMEM((ROWS, F6), bf16),
            pltpu.VMEM((ROWS, F6), bf16),
            pltpu.VMEM((768, F6), bf16),
            dma((LANES,)),
            dma((LANES,)),
            dma((LANES,)),
            dma((LANES,)),
            dma((LANES,)),
            dma((LANES,)),
            dma((3, LANES)),
            dma((10,)),
            dma((10,)),
            dma((5,)),
            dma((5,)),
            dma((2,)),
        ],
        compiler_params=pltpu.CompilerParams(
            collective_id=0, has_side_effects=True, vmem_limit_bytes=54528 * 1024
        ),
    )(
        jnp.transpose(positions, (1, 0, 2)),
        masses,
        block_owner.T,
        block_oct[None, :],
        jnp.transpose(face_owner, (1, 2, 0)),
        face_oct.T,
        face_coarse.T,
        face_quadrant.T,
    )
    return potential, jnp.transpose(accel, (1, 0, 2))


def solution(mesh):
    placed = (
        P("hilbert", None, None),
        P("hilbert", None),
        P("hilbert", None),
        P("hilbert"),
        P("hilbert", None, None),
        P("hilbert", None),
        P("hilbert", None),
        P("hilbert", None),
    )
    return jax.shard_map(
        on_device,
        mesh=mesh,
        in_specs=placed,
        out_specs=(P("hilbert", None), P("hilbert", None, None)),
        check_vma=False,
    )
```
